32 devices in a mesh: groups: 2 (over x), blk: 16 (over z, y, core).
Axes of the slice: x: 2, y: 2, z: 4, core: 2. Of those that a mesh axis runs over, the one named last changes fastest.
Arguments:
- tokens: bfloat16 [4096, 8192], P(('groups', 'blk')), parts along dimension 0, may hold values from -6 to 6
- cotangent: bfloat16 [4096, 8192], P(('groups', 'blk')), parts along dimension 0, may hold values from -6 to 6
- tenant: int32 [4096, 1], P(('groups', 'blk')), parts along dimension 0, may hold values from 0 to 15; in each aligned block of 128 rows (0 to 127, 128 to 255, ...) at most 16 rows name the same one
- owner: int32 [32], P('groups'), parts along dimension 0, may hold values from 0 to 15, each once
- down_factor_table: bfloat16 [32, 64, 8192], P(('groups', 'blk')), parts along dimension 0, may hold values from -0.0625 to 0.0625
- up_factor_table: bfloat16 [32, 64, 8192], P(('groups', 'blk')), parts along dimension 0, may hold values from -0.0625 to 0.0625
Outputs:
- input_grad: bfloat16 [4096, 8192], P(('groups', 'blk')), parts along dimension 0
- grad_a: bfloat16 [32, 64, 8192], P(('groups', 'blk')), parts along dimension 0
- grad_b: bfloat16 [32, 64, 8192], P(('groups', 'blk')), parts along dimension 0
The draws below stay inside these ranges and needn't reach their ends.
There are 2 independent parts, one for each index of `groups`. The reference program is written for one: setup_inputs(seed, part) draws one part's arguments, and reference() takes and returns one part's arrays. A program takes and returns all parts, laid end to end along the dimension named above; each array names one. Nothing has to cross between parts.
Inputs may be any that keep to these rules, and one draw needn't show every extreme that they name: No tenant is named by more than 16 rows of one device; some tenant reaches 16 rows of some device; every tenant is named by some row. `owner`: each storage index appears once.
All inputs are finite; a program needn't handle non-finite values.
Results may differ from the reference program's by a relative error of at most 0.0049.
Values may be sent and summed in bfloat16 or wider, within the bound.
No kernel may reach another device: no remote copies, remote signals or barrier semaphores. Data moves between devices by JAX's collectives and lax.ppermute only.
A program may use at most 128 MiB of HBM per device.

```python
import math
import jax
import jax.numpy as jnp
import numpy as np
from jax import lax

MODEL_WIDTH = 8192
ADAPTER_RANK = 64
TOK_DEV = 128
GROUP_ADAPTERS = 16
CAP = 16
TOKENS = 2048
N_BLK = 16


def block_levels(rng, shape, shards, low, top_value):
    gain = 1.0
    for axis_at, parts in shards:
        draws = jax.random.uniform(jax.random.fold_in(jax.random.fold_in(rng, 6), axis_at), (parts,), jnp.float32, low / len(shards), top_value / len(shards))
        gain = gain * jnp.repeat(jnp.exp(draws), shape[axis_at] // parts).reshape((-1,) + (1,) * (len(shape) - 1 - axis_at))
    return gain


def shared_out(rng, own, number, rows, number_of, top, limit, lean):
    ranking = jax.random.permutation(rng, number_of)
    packed, ordinary = shares(number_of, rows * top, limit, lean, True), shares(number_of, rows * top, limit, lean, False)
    places = jnp.arange(number_of)

    def named(lengths, rotation):
        used = int((lengths > 0).sum())
        fixed = max(1, used // 4)
        shifted = fixed + (places - fixed + rotation * (used - fixed)) % max(1, number_of - fixed)
        return jnp.zeros((number_of,), jnp.int32).at[ranking[jnp.where(places < fixed, places, shifted)]].set(jnp.asarray(lengths, jnp.int32))

    lengths = jnp.where(number % 4 == 0, named(packed, number // 4), named(ordinary, number - number // 4 - 1))
    mixed = jax.random.permutation(jax.random.fold_in(own, 3), number_of)
    donor, sink = mixed[0:number_of // 2 * 2:2], mixed[1:number_of // 2 * 2:2]
    room = jnp.minimum(lengths[donor] - 1, limit - lengths[sink]) // 2
    room = jnp.where((donor == ranking[0]) | (sink == ranking[0]) | (lengths[sink] == 0), 0, jnp.maximum(room, 0))
    shifted = jax.random.randint(jax.random.fold_in(own, 4), (number_of // 2,), 0, 1 << 20) % (room + 1)
    lengths = lengths.at[donor].add(-shifted).at[sink].add(shifted)
    items = jnp.searchsorted(jnp.cumsum(lengths), jnp.arange(rows * top), side="right").astype(jnp.int32)
    table = items.reshape(top, rows).T
    table = table[jax.random.permutation(jax.random.fold_in(own, 1), rows)]
    rotation = jax.random.randint(jax.random.fold_in(own, 2), (rows, 1), 0, top)
    return jnp.take_along_axis(table, (jnp.arange(top)[None, :] + rotation) % top, axis=1)


def shares(number_of, total, bound, lean, full):
    portions = [(1 << 20) // math.isqrt(rank ** lean) + 1 for rank in range(1, number_of + 1)]
    largest = bound if full else min(bound, max(-(-total // number_of), total * portions[0] // sum(portions)))
    least = 1 if total - largest >= number_of - 1 else 0
    given, spare = [largest] + [least] * (number_of - 1), total - largest - least * (number_of - 1)
    while spare > 0:
        free = [i for i in range(1, number_of) if given[i] < largest] or [i for i in range(1, number_of) if given[i] < bound]
        whole, remaining = sum([portions[i] for i in free]), spare
        for i in free:
            extra = min(bound - given[i], max(1, remaining * portions[i] // whole), spare)
            given[i] = given[i] + extra
            spare = spare - extra
    return np.array(given)


def centred(key, shape, scale, limit, cuts=(), held_as=jnp.bfloat16):
    factor_of = block_levels(key, shape, cuts, -0.22, 0.18) if cuts else 1.0
    entries = jax.random.normal(key, shape, jnp.float32) * scale * factor_of
    return jnp.minimum(jnp.maximum(entries, -limit), limit).astype(held_as)


def setup_inputs(seed: int = 0, part: int = 0) -> dict:
    streams_of = jax.random.split(jax.random.key(seed), 7)
    part_keys = jax.random.split(jax.random.fold_in(streams_of[6], part), 7)
    tokens = centred(part_keys[0], (TOKENS, MODEL_WIDTH), 1.0, 6.0, ((0, 16),))
    cotangent = centred(part_keys[1], (TOKENS, MODEL_WIDTH), 1.0, 6.0, ((0, 16),))
    tenant_keys = jax.random.split(jax.random.fold_in(part_keys[2], 1), TOKENS // TOK_DEV)
    tenant_turns = jax.random.permutation(jax.random.fold_in(part_keys[2], 3), TOKENS // TOK_DEV)
    tenant = jax.vmap(lambda own, number: shared_out(jax.random.fold_in(part_keys[2], 2), own, number, TOK_DEV, GROUP_ADAPTERS, 1, CAP, 2))(tenant_keys, tenant_turns).reshape((TOKENS, 1))
    owner = jax.random.permutation(part_keys[3], GROUP_ADAPTERS).astype(jnp.int32)
    down_factor_table = centred(part_keys[4], (GROUP_ADAPTERS, ADAPTER_RANK, MODEL_WIDTH), MODEL_WIDTH ** -0.5, 0.0625, ((0, 16),))
    up_factor_table = centred(part_keys[5], (GROUP_ADAPTERS, ADAPTER_RANK, MODEL_WIDTH), MODEL_WIDTH ** -0.5, 0.0625, ((0, 16),))
    return {"tokens": tokens, "cotangent": cotangent, "tenant": tenant, "owner": owner, "down_factor_table": down_factor_table, "up_factor_table": up_factor_table}


SCALE = 2.0
DAMPING = 1.0
EPS = 1e-06

def project(grad, left, right):
    top = jnp.dot(left, grad, precision=lax.Precision.HIGHEST)
    inner = grad - left[:, None] * top[None, :] / (DAMPING + jnp.sum(left * left))
    side = jnp.dot(inner, right, precision=lax.Precision.HIGHEST)
    return inner - side[:, None] * right[None, :] / (DAMPING + jnp.sum(right * right))

def reference(tokens, cotangent, tenant, owner, down_factor_table, up_factor_table):
    total_rows = tokens.shape[0]
    width = tokens.shape[1]
    rank_position = down_factor_table.shape[1]
    block = N_BLK * CAP
    slot_of_row = owner[tenant[:, 0]].astype(jnp.int32)
    order = jnp.argsort(slot_of_row, stable=True).astype(jnp.int32)
    counts = jnp.zeros((GROUP_ADAPTERS,), jnp.int32).at[slot_of_row].add(1)
    starts = (jnp.cumsum(counts) - counts).astype(jnp.int32)
    padding = jnp.zeros((block, width), tokens.dtype)
    sorted_x = jnp.concatenate([tokens[order], padding], 0)
    sorted_dy = jnp.concatenate([cotangent[order], padding], 0)
    positions = jnp.arange(block, dtype=jnp.int32)
    dims = (((1,), (1,)), ((), ()))
    rows_dims = (((0,), (0,)), ((), ()))

    def step(carry, storage_slot):
        start = starts[storage_slot]
        number = counts[storage_slot]
        live = (positions < number)[:, None]
        zero = jnp.zeros((), tokens.dtype)
        rows_x = jnp.where(live, lax.dynamic_slice_in_dim(sorted_x, start, block, 0), zero)
        rows_dy = jnp.where(live, lax.dynamic_slice_in_dim(sorted_dy, start, block, 0), zero)
        down_weight = down_factor_table[storage_slot]
        up_weight = up_factor_table[storage_slot]
        hidden = lax.dot_general(rows_x, down_weight, dims, preferred_element_type=jnp.float32).astype(jnp.bfloat16)
        grad_hidden = (SCALE * lax.dot_general(rows_dy, up_weight, dims, preferred_element_type=jnp.float32)).astype(jnp.bfloat16)
        back = jnp.dot(grad_hidden, down_weight, preferred_element_type=jnp.float32).astype(jnp.bfloat16)
        raw_a = lax.dot_general(grad_hidden, rows_x, rows_dims, preferred_element_type=jnp.float32)
        raw_b = SCALE * lax.dot_general(hidden, rows_dy, rows_dims, preferred_element_type=jnp.float32)
        amount = number.astype(jnp.float32)
        xbar = lax.optimization_barrier(jnp.sum(rows_x, axis=0, dtype=jnp.float32)) / amount
        ybar = lax.optimization_barrier(jnp.sum(rows_dy, axis=0, dtype=jnp.float32)) / amount
        hbar = lax.optimization_barrier(jnp.sum(hidden, axis=0, dtype=jnp.float32)) / amount
        gbar = lax.optimization_barrier(jnp.sum(grad_hidden, axis=0, dtype=jnp.float32)) / amount
        proj_a = project(raw_a, gbar, xbar)
        proj_b = project(raw_b, hbar, ybar)
        old = lax.dynamic_slice_in_dim(carry, start, block, 0)
        carry = lax.dynamic_update_slice_in_dim(carry, jnp.where(live, back, old), start, 0)
        return (carry, (proj_a, proj_b))
    start_rows = jnp.zeros((total_rows + block, width), jnp.bfloat16)
    out_sorted, (proj_a, proj_b) = lax.scan(step, start_rows, jnp.arange(GROUP_ADAPTERS, dtype=jnp.int32))
    input_grad = jnp.zeros((total_rows, width), jnp.bfloat16).at[order].set(out_sorted[:total_rows])
    total = jnp.sum(proj_a * proj_a) + jnp.sum(proj_b * proj_b)
    mean_sq = total / (2.0 * GROUP_ADAPTERS * rank_position * width)
    factor = jnp.minimum(1.0, 1.0 / jnp.sqrt(mean_sq + EPS))
    return (input_grad, (factor * proj_a).astype(jnp.bfloat16), (factor * proj_b).astype(jnp.bfloat16))
```

```python
import jax
import jax.numpy as jnp
from jax import lax
from jax.experimental import pallas as pl
from jax.experimental.pallas import tpu as pltpu
from jax.sharding import PartitionSpec as P

SCALE = 2.0
DAMPING = 1.0
EPS = 1e-06
VMEM_LIMIT = 48 * 1024 * 1024
LAST = (((1,), (1,)), ((), ()))
FIRST = (((0,), (0,)), ((), ()))


def total_over_blk(value):
    size = lax.axis_size("blk")
    if size & (size - 1):
        return lax.psum(value, "blk")
    step = 1
    while step < size:
        value = value + lax.ppermute(value, "blk", [(i, i ^ step) for i in range(size)])
        step *= 2
    return value


def rows_kernel(scale, rows_ref, weight_ref, low_ref, gram_ref, low_total):
    step = pl.program_id(0)

    @pl.when(step == 0)
    def _():
        low_total[...] = jnp.zeros_like(low_total)
        gram_ref[...] = jnp.zeros_like(gram_ref)

    rows = rows_ref[...]
    low_total[...] += lax.dot_general(rows, weight_ref[...], LAST, preferred_element_type=jnp.float32)
    gram_ref[...] += lax.dot_general(rows, rows, LAST, preferred_element_type=jnp.float32)

    @pl.when(step == pl.num_programs(0) - 1)
    def _():
        low_ref[...] = (scale * low_total[...]).astype(low_ref.dtype)


def rows_products(rows, weight, scale):
    slots, width = rows.shape
    rank = weight.shape[0]
    chunk = min(width, 2048)
    return pl.pallas_call(
        lambda *refs: rows_kernel(scale, *refs),
        grid=(width // chunk,),
        in_specs=[
            pl.BlockSpec((slots, chunk), lambda i: (0, i)),
            pl.BlockSpec((rank, chunk), lambda i: (0, i)),
        ],
        out_specs=[
            pl.BlockSpec((slots, rank), lambda i: (0, 0)),
            pl.BlockSpec((slots, slots), lambda i: (0, 0)),
        ],
        out_shape=[
            jax.ShapeDtypeStruct((slots, rank), jnp.bfloat16),
            jax.ShapeDtypeStruct((slots, slots), jnp.float32),
        ],
        scratch_shapes=[pltpu.VMEM((slots, rank), jnp.float32)],
        compiler_params=pltpu.CompilerParams(vmem_limit_bytes=VMEM_LIMIT),
        cost_estimate=pl.CostEstimate(
            flops=2 * slots * width * (slots + rank),
            bytes_accessed=2 * width * (slots + rank),
            transcendentals=0,
        ),
    )(rows, weight)


def fold_one(low, gram, scale, amount):
    high = lax.Precision.HIGHEST
    low = low.astype(jnp.float32)
    slots = low.shape[0]
    left = jnp.sum(low, axis=0, keepdims=True) / amount
    raw = scale * low
    along = jnp.sum(raw * left, axis=1, keepdims=True)
    inner = raw - along * left / (DAMPING + jnp.sum(left * left))
    cross = jnp.sum(gram, axis=1, keepdims=True) / amount
    right_sq = jnp.sum(cross) / amount
    side = jnp.sum(inner * cross, axis=0, keepdims=True)
    factor = inner - side / (amount * (DAMPING + right_sq))
    spread = jnp.dot(gram, factor, precision=high, preferred_element_type=jnp.float32)
    return factor, jnp.sum(spread * factor)


def split3(value):
    first = value.astype(jnp.bfloat16)
    rest = value - first.astype(jnp.float32)
    second = rest.astype(jnp.bfloat16)
    third = (rest - second.astype(jnp.float32)).astype(jnp.bfloat16)
    return first, second, third


def fold_kernel(amount_ref, gh_ref, gram_x_ref, hidden_ref, gram_dy_ref, left_a_ref, left_b_ref, sq_ref):
    amount = amount_ref[0, 0]
    rank = gh_ref.shape[1]
    factor_a, sq_a = fold_one(gh_ref[...], gram_x_ref[...], 1.0, amount)
    factor_b, sq_b = fold_one(hidden_ref[...], gram_dy_ref[...], SCALE, amount)
    for out_ref, factor in ((left_a_ref, factor_a), (left_b_ref, factor_b)):
        for at, part in enumerate(split3(factor)):
            out_ref[:, at * rank : (at + 1) * rank] = part
    sq_ref[...] = jnp.zeros_like(sq_ref) + (sq_a + sq_b)


def fold(amount, grad_hidden, gram_x, hidden, gram_dy):
    slots, rank = hidden.shape
    whole = lambda shape: pl.BlockSpec(shape, lambda: (0, 0))
    return pl.pallas_call(
        fold_kernel,
        in_specs=[pl.BlockSpec(memory_space=pltpu.SMEM)]
        + [whole((slots, rank)), whole((slots, slots))] * 2,
        out_specs=[whole((slots, 3 * rank))] * 2 + [whole((8, 128))],
        out_shape=[jax.ShapeDtypeStruct((slots, 3 * rank), jnp.bfloat16)] * 2
        + [jax.ShapeDtypeStruct((8, 128), jnp.float32)],
        compiler_params=pltpu.CompilerParams(vmem_limit_bytes=VMEM_LIMIT),
        cost_estimate=pl.CostEstimate(
            flops=24 * slots * slots * rank, bytes_accessed=12 * slots * slots, transcendentals=0
        ),
    )(amount, grad_hidden, gram_x, hidden, gram_dy)


def grads_kernel(factor_ref, left_a_ref, left_b_ref, rows_x_ref, rows_dy_ref, grad_a_ref, grad_b_ref):
    factor = factor_ref[0, 0]
    rank = grad_a_ref.shape[0]
    for left_ref, rows_ref, out_ref in (
        (left_a_ref, rows_x_ref, grad_a_ref),
        (left_b_ref, rows_dy_ref, grad_b_ref),
    ):
        parts = lax.dot_general(left_ref[...], rows_ref[...], FIRST, preferred_element_type=jnp.float32)
        proj = (parts[2 * rank :] + parts[rank : 2 * rank]) + parts[:rank]
        out_ref[...] = (factor * proj).astype(out_ref.dtype)


def grads(factor, left_a, left_b, rows_x, rows_dy):
    slots, width = rows_x.shape
    rank = left_a.shape[1] // 3
    chunk = min(width, 2048)
    left_spec = pl.BlockSpec((slots, 3 * rank), lambda i: (0, 0))
    rows_spec = pl.BlockSpec((slots, chunk), lambda i: (0, i))
    out_spec = pl.BlockSpec((rank, chunk), lambda i: (0, i))
    return pl.pallas_call(
        grads_kernel,
        grid=(width // chunk,),
        in_specs=[pl.BlockSpec(memory_space=pltpu.SMEM), left_spec, left_spec, rows_spec, rows_spec],
        out_specs=[out_spec, out_spec],
        out_shape=[jax.ShapeDtypeStruct((rank, width), jnp.bfloat16)] * 2,
        compiler_params=pltpu.CompilerParams(vmem_limit_bytes=VMEM_LIMIT),
        cost_estimate=pl.CostEstimate(
            flops=12 * slots * width * rank, bytes_accessed=4 * width * (slots + rank), transcendentals=0
        ),
    )(factor, left_a, left_b, rows_x, rows_dy)


def per_device(tokens, cotangent, tenant, owner, down_factor_table, up_factor_table):
    rows, width = tokens.shape
    count_blk = lax.axis_size("blk")
    adapters = owner.shape[0]
    rank = down_factor_table.shape[1]
    cap = 2 * rows // adapters
    slots = count_blk * cap
    down_weight = down_factor_table[0]
    up_weight = up_factor_table[0]

    with jax.named_scope("targets"):
        tenant_ids = tenant[:, 0]
        match = tenant_ids[:, None] == jnp.arange(adapters, dtype=jnp.int32)[None, :]
        target_dev = jnp.sum(jnp.where(match, owner[None, :], 0), axis=1)
        row_ids = jnp.arange(rows, dtype=jnp.int32)
        same_before = (tenant_ids[:, None] == tenant_ids[None, :]) & (row_ids[None, :] < row_ids[:, None])
        position = jnp.sum(same_before.astype(jnp.int32), axis=1)
        target = target_dev * cap + position
        placing = (jnp.arange(slots, dtype=jnp.int32)[:, None] == target[None, :]).astype(jnp.bfloat16)

    def exchange(value):
        value = value.reshape(count_blk, cap, width)
        return lax.all_to_all(value, "blk", split_axis=0, concat_axis=0, tiled=True).reshape(slots, width)

    def place(value):
        return jnp.dot(placing, value, preferred_element_type=jnp.float32).astype(jnp.bfloat16)

    with jax.named_scope("send_cotangent"):
        rows_dy = exchange(place(cotangent))
    with jax.named_scope("send_tokens"):
        rows_x = exchange(place(tokens))
    with jax.named_scope("row_counts"):
        devices = jnp.arange(count_blk, dtype=jnp.int32)
        sent = jnp.sum((target_dev[:, None] == devices[None, :]).astype(jnp.float32), axis=0, keepdims=True)
        counts = total_over_blk(sent)
        amount = jnp.sum(jnp.where(devices == lax.axis_index("blk"), counts[0], 0.0)).reshape(1, 1)
    with jax.named_scope("grad_hidden"):
        grad_hidden, gram_dy = rows_products(rows_dy, up_weight, SCALE)
    with jax.named_scope("back"):
        back = jnp.dot(grad_hidden, down_weight, preferred_element_type=jnp.float32).astype(jnp.bfloat16)
        returned = exchange(back)
    with jax.named_scope("hidden"):
        hidden, gram_x = rows_products(rows_x, down_weight, 1.0)
    with jax.named_scope("fold"):
        left_a, left_b, local_sq = fold(amount, grad_hidden, gram_x, hidden, gram_dy)
    with jax.named_scope("clip"):
        total = total_over_blk(local_sq[:1, :1])
        mean_sq = total / (2.0 * adapters * rank * width)
        factor = jnp.minimum(1.0, 1.0 / jnp.sqrt(mean_sq + EPS))
    with jax.named_scope("grads"):
        grad_a, grad_b = grads(factor, left_a, left_b, rows_x, rows_dy)
    with jax.named_scope("input_grad"):
        input_grad = lax.dot_general(placing, returned, FIRST, preferred_element_type=jnp.float32).astype(
            jnp.bfloat16
        )
    return (input_grad, grad_a[None], grad_b[None])


def solution(mesh):
    split = ("groups", "blk")
    in_specs = (P(split, None), P(split, None), P(split, None), P("groups"), P(split, None, None), P(split, None, None))
    out_specs = (P(split, None), P(split, None, None), P(split, None, None))
    return jax.shard_map(per_device, mesh=mesh, in_specs=in_specs, out_specs=out_specs, check_vma=False)
```

```python
import jax
import jax.numpy as jnp
from jax import lax
from jax.experimental import pallas as pl
from jax.experimental.pallas import tpu as pltpu
from jax.sharding import PartitionSpec as P

SCALE = 2.0
DAMPING = 1.0
EPS = 1e-06
VMEM_LIMIT = 48 * 1024 * 1024
LANES = 128
LAST = (((1,), (1,)), ((), ()))
FIRST = (((0,), (0,)), ((), ()))


def total_over_blk(value):
    size = lax.axis_size("blk")
    if size & (size - 1):
        return lax.psum(value, "blk")
    step = 1
    while step < size:
        value = value + lax.ppermute(value, "blk", [(i, i ^ step) for i in range(size)])
        step *= 2
    return value


def rows_kernel(scale, count, with_extra, *refs):
    blocks, extras = refs[:count], refs[count : 2 * count if with_extra else count]
    weight_ref, low_ref, gram_ref, *rest = refs[count + len(extras) :]
    low_total = rest[-1]
    step = pl.program_id(0)

    @pl.when(step == 0)
    def _():
        low_total[...] = jnp.zeros_like(low_total)
        gram_ref[...] = jnp.zeros_like(gram_ref)
        if with_extra:
            rest[0][...] = jnp.concatenate([ref[...] for ref in extras], axis=0)

    rows = jnp.concatenate([ref[...] for ref in blocks], axis=0)
    low_total[...] += lax.dot_general(rows, weight_ref[...], LAST, preferred_element_type=jnp.float32)
    gram_ref[...] += lax.dot_general(rows, rows, LAST, preferred_element_type=jnp.float32)

    @pl.when(step == pl.num_programs(0) - 1)
    def _():
        low_ref[...] = (scale * low_total[...]).astype(low_ref.dtype)


def rows_products(blocks, weight, scale, with_extra=False):
    slots = sum(block.shape[0] for block in blocks)
    rank, width = weight.shape
    chunk = min(width, 2048)
    in_specs = [pl.BlockSpec((block.shape[0], chunk), lambda i: (0, i)) for block in blocks]
    out_specs = [pl.BlockSpec((slots, rank), lambda i: (0, 0)), pl.BlockSpec((slots, slots), lambda i: (0, 0))]
    out_shape = [
        jax.ShapeDtypeStruct((slots, rank), jnp.bfloat16),
        jax.ShapeDtypeStruct((slots, slots), jnp.float32),
    ]
    operands = list(blocks)
    if with_extra:
        in_specs += [pl.BlockSpec((block.shape[0], LANES), lambda i: (0, width // LANES)) for block in blocks]
        operands += list(blocks)
        out_specs.append(pl.BlockSpec((slots, LANES), lambda i: (0, 0)))
        out_shape.append(jax.ShapeDtypeStruct((slots, LANES), jnp.bfloat16))
    return pl.pallas_call(
        lambda *refs: rows_kernel(scale, len(blocks), with_extra, *refs),
        grid=(width // chunk,),
        in_specs=in_specs + [pl.BlockSpec((rank, chunk), lambda i: (0, i))],
        out_specs=out_specs,
        out_shape=out_shape,
        scratch_shapes=[pltpu.VMEM((slots, rank), jnp.float32)],
        compiler_params=pltpu.CompilerParams(vmem_limit_bytes=VMEM_LIMIT),
        cost_estimate=pl.CostEstimate(
            flops=2 * slots * width * (slots + rank),
            bytes_accessed=2 * width * (slots + rank),
            transcendentals=0,
        ),
    )(*operands, weight)


def low_kernel(scale, count, *refs):
    blocks, weight_ref, low_ref, total = refs[:count], *refs[count:]
    step = pl.program_id(0)

    @pl.when(step == 0)
    def _():
        total[...] = jnp.zeros_like(total)

    rows = jnp.concatenate([ref[...] for ref in blocks], axis=0)
    total[...] += lax.dot_general(rows, weight_ref[...], LAST, preferred_element_type=jnp.float32)

    @pl.when(step == pl.num_programs(0) - 1)
    def _():
        low_ref[...] = (scale * total[...]).astype(low_ref.dtype)


def low_products(blocks, weight, scale):
    slots = sum(block.shape[0] for block in blocks)
    rank, width = weight.shape
    chunk = min(width, 2048)
    return pl.pallas_call(
        lambda *refs: low_kernel(scale, len(blocks), *refs),
        grid=(width // chunk,),
        in_specs=[pl.BlockSpec((block.shape[0], chunk), lambda i: (0, i)) for block in blocks]
        + [pl.BlockSpec((rank, chunk), lambda i: (0, i))],
        out_specs=pl.BlockSpec((slots, rank), lambda i: (0, 0)),
        out_shape=jax.ShapeDtypeStruct((slots, rank), jnp.bfloat16),
        scratch_shapes=[pltpu.VMEM((slots, rank), jnp.float32)],
        compiler_params=pltpu.CompilerParams(vmem_limit_bytes=VMEM_LIMIT),
        cost_estimate=pl.CostEstimate(
            flops=2 * slots * width * rank, bytes_accessed=2 * width * (slots + rank), transcendentals=0
        ),
    )(*blocks, weight)


def slot_targets(cap, me, owner_ref, column_ref, row_ref):
    column, row = column_ref[...], row_ref[...]
    rows, adapters = row.shape[1], owner_ref.shape[0]
    adapter = lax.broadcasted_iota(jnp.int32, (adapters, rows), 0)
    device = jnp.sum(jnp.where(adapter == row, owner_ref[...], 0), axis=0, keepdims=True)
    earlier = lax.broadcasted_iota(jnp.int32, (rows, rows), 0) < lax.broadcasted_iota(jnp.int32, (rows, rows), 1)
    position = jnp.sum(jnp.where((column == row) & earlier, 1, 0), axis=0, keepdims=True)
    partner = device ^ me
    return partner, partner * cap + position


def place_kernel(partners, cap, with_extra, me_ref, owner_ref, column_ref, row_ref, values_ref, *refs):
    placing = refs[-1]
    outs = refs[1:-1] if with_extra else refs[:-1]
    step = pl.program_id(0)
    rows = row_ref.shape[1]

    @pl.when(step == 0)
    def _():
        _, target = slot_targets(cap, me_ref[0, 0], owner_ref, column_ref, row_ref)
        slot = lax.broadcasted_iota(jnp.int32, (cap, rows), 0)
        for at, partner in enumerate(partners):
            placing[at * cap : (at + 1) * cap, :] = jnp.where(slot + partner * cap == target, 1.0, 0.0).astype(
                placing.dtype
            )

    placed = jnp.dot(placing[...], values_ref[...], preferred_element_type=jnp.float32).astype(jnp.bfloat16)
    for at, out in enumerate(outs):
        out[...] = placed[at * cap : (at + 1) * cap]

    if with_extra:

        @pl.when(step == pl.num_programs(0) - 1)
        def _():
            live = jnp.sum(placing[...].astype(jnp.float32), axis=1, keepdims=True)
            low = refs[0][...].astype(jnp.float32)
            extra = jnp.concatenate(
                [low, jnp.broadcast_to(live, (live.shape[0], LANES - low.shape[1]))], axis=1
            ).astype(jnp.bfloat16)
            for at, out in enumerate(outs):
                out[:, out.shape[1] - LANES :] = extra[at * cap : (at + 1) * cap]


def place(partners, cap, me, owner, tenant, values, low=None):
    rows, width = values.shape
    adapters = owner.shape[0]
    with_extra = low is not None
    full = width + LANES if with_extra else width
    chunk = full // 5 if with_extra and full % (5 * LANES) == 0 else 2048
    still = lambda shape: pl.BlockSpec(shape, lambda i: (0, 0))
    in_specs = [
        pl.BlockSpec(memory_space=pltpu.SMEM),
        still((adapters, 1)),
        still((rows, 1)),
        still((1, rows)),
        pl.BlockSpec((rows, chunk), lambda i: (0, i)),
    ]
    operands = [me.reshape(1, 1), owner.reshape(adapters, 1), tenant, tenant.reshape(1, rows), values]
    if with_extra:
        in_specs.append(still(low.shape))
        operands.append(low)
    return pl.pallas_call(
        lambda *refs: place_kernel(partners, cap, with_extra, *refs),
        grid=(full // chunk,),
        in_specs=in_specs,
        out_specs=[pl.BlockSpec((cap, chunk), lambda i: (0, i))] * len(partners),
        out_shape=[jax.ShapeDtypeStruct((cap, full), jnp.bfloat16)] * len(partners),
        scratch_shapes=[pltpu.VMEM((len(partners) * cap, rows), jnp.bfloat16)],
        compiler_params=pltpu.CompilerParams(vmem_limit_bytes=VMEM_LIMIT),
        cost_estimate=pl.CostEstimate(
            flops=2 * len(partners) * cap * rows * width,
            bytes_accessed=2 * width * (rows + len(partners) * cap),
            transcendentals=0,
        ),
    )(*operands)


def input_grad_kernel(cap, count, me_ref, owner_ref, column_ref, row_ref, partner_ref, extra_ref, *refs):
    pieces, out_ref, left = refs[:count], refs[count], refs[count + 1]
    step = pl.program_id(0)
    rows, slots = row_ref.shape[1], extra_ref.shape[0]
    rank = pieces[0].shape[0]

    @pl.when(step == 0)
    def _():
        partner, target = slot_targets(cap, me_ref[0, 0], owner_ref, column_ref, row_ref)
        slot = lax.broadcasted_iota(jnp.int32, (slots, rows), 0)
        for at in range(count):
            picked = jnp.where((slot == target) & (partner == partner_ref[at]), 1.0, 0.0).astype(jnp.bfloat16)
            low = lax.dot_general(picked, extra_ref[:, :rank], FIRST, preferred_element_type=jnp.float32)
            left[:, at * rank : (at + 1) * rank] = low.astype(left.dtype)

    stacked = jnp.concatenate([ref[...] for ref in pieces], axis=0)
    out_ref[...] = jnp.dot(left[...], stacked, preferred_element_type=jnp.float32).astype(out_ref.dtype)


def input_grad_of(cap, me, owner, tenant, partners, extra, pieces):
    rows, adapters, slots = tenant.shape[0], owner.shape[0], extra.shape[0]
    rank, width = pieces[0].shape
    count = len(pieces)
    chunk = min(width, 1024)
    still = lambda shape: pl.BlockSpec(shape, lambda i: (0, 0))
    return pl.pallas_call(
        lambda *refs: input_grad_kernel(cap, count, *refs),
        grid=(width // chunk,),
        in_specs=[
            pl.BlockSpec(memory_space=pltpu.SMEM),
            still((adapters, 1)),
            still((rows, 1)),
            still((1, rows)),
            pl.BlockSpec(memory_space=pltpu.SMEM),
            still((slots, LANES)),
        ]
        + [pl.BlockSpec((rank, chunk), lambda i: (0, i))] * count,
        out_specs=pl.BlockSpec((rows, chunk), lambda i: (0, i)),
        out_shape=jax.ShapeDtypeStruct((rows, width), jnp.bfloat16),
        scratch_shapes=[pltpu.VMEM((rows, count * rank), jnp.bfloat16)],
        compiler_params=pltpu.CompilerParams(vmem_limit_bytes=VMEM_LIMIT),
        cost_estimate=pl.CostEstimate(
            flops=2 * rows * count * rank * width,
            bytes_accessed=2 * width * (rows + count * rank),
            transcendentals=0,
        ),
    )(me.reshape(1, 1), owner.reshape(adapters, 1), tenant, tenant.reshape(1, rows), partners, extra, *pieces)


def fold_one(low, gram, scale, amount):
    high = lax.Precision.HIGHEST
    low = low.astype(jnp.float32)
    slots = low.shape[0]
    left = jnp.sum(low, axis=0, keepdims=True) / amount
    raw = scale * low
    along = jnp.sum(raw * left, axis=1, keepdims=True)
    inner = raw - along * left / (DAMPING + jnp.sum(left * left))
    cross = jnp.sum(gram, axis=1, keepdims=True) / amount
    right_sq = jnp.sum(cross) / amount
    side = jnp.sum(inner * cross, axis=0, keepdims=True)
    factor = inner - side / (amount * (DAMPING + right_sq))
    spread = jnp.dot(gram, factor, precision=high, preferred_element_type=jnp.float32)
    return factor, jnp.sum(spread * factor)


def split3(value):
    first = value.astype(jnp.bfloat16)
    rest = value - first.astype(jnp.float32)
    second = rest.astype(jnp.bfloat16)
    third = (rest - second.astype(jnp.float32)).astype(jnp.bfloat16)
    return first, second, third


def fold_kernel(amount_ref, gh_ref, gram_x_ref, hidden_ref, gram_dy_ref, left_a_ref, left_b_ref, sq_ref):
    amount = amount_ref[0, 0]
    rank = gh_ref.shape[1]
    factor_a, sq_a = fold_one(gh_ref[...], gram_x_ref[...], 1.0, amount)
    factor_b, sq_b = fold_one(hidden_ref[...], gram_dy_ref[...], SCALE, amount)
    for out_ref, factor in ((left_a_ref, factor_a), (left_b_ref, factor_b)):
        for at, part in enumerate(split3(factor)):
            out_ref[:, at * rank : (at + 1) * rank] = part
    sq_ref[...] = jnp.zeros_like(sq_ref) + (sq_a + sq_b)


def fold(amount, grad_hidden, gram_x, hidden, gram_dy):
    slots, rank = hidden.shape
    whole = lambda shape: pl.BlockSpec(shape, lambda: (0, 0))
    return pl.pallas_call(
        fold_kernel,
        in_specs=[pl.BlockSpec(memory_space=pltpu.SMEM)]
        + [whole((slots, rank)), whole((slots, slots))] * 2,
        out_specs=[whole((slots, 3 * rank))] * 2 + [whole((8, 128))],
        out_shape=[jax.ShapeDtypeStruct((slots, 3 * rank), jnp.bfloat16)] * 2
        + [jax.ShapeDtypeStruct((8, 128), jnp.float32)],
        compiler_params=pltpu.CompilerParams(vmem_limit_bytes=VMEM_LIMIT),
        cost_estimate=pl.CostEstimate(
            flops=24 * slots * slots * rank, bytes_accessed=12 * slots * slots, transcendentals=0
        ),
    )(amount, grad_hidden, gram_x, hidden, gram_dy)


def grads_kernel(count, factor_ref, left_a_ref, left_b_ref, *refs):
    blocks_x, blocks_dy = refs[:count], refs[count : 2 * count]
    grad_a_ref, grad_b_ref = refs[2 * count :]
    factor = factor_ref[0, 0]
    rank = grad_a_ref.shape[0]
    for left_ref, blocks, out_ref in ((left_a_ref, blocks_x, grad_a_ref), (left_b_ref, blocks_dy, grad_b_ref)):
        rows = jnp.concatenate([ref[...] for ref in blocks], axis=0)
        parts = lax.dot_general(left_ref[...], rows, FIRST, preferred_element_type=jnp.float32)
        proj = (parts[2 * rank :] + parts[rank : 2 * rank]) + parts[:rank]
        out_ref[...] = (factor * proj).astype(out_ref.dtype)


def grads(factor, left_a, left_b, blocks_x, blocks_dy, width):
    slots = left_a.shape[0]
    rank = left_a.shape[1] // 3
    chunk = min(width, 2048)
    left_spec = pl.BlockSpec((slots, 3 * rank), lambda i: (0, 0))
    rows_specs = [pl.BlockSpec((block.shape[0], chunk), lambda i: (0, i)) for block in blocks_x]
    out_spec = pl.BlockSpec((rank, chunk), lambda i: (0, i))
    return pl.pallas_call(
        lambda *refs: grads_kernel(len(blocks_x), *refs),
        grid=(width // chunk,),
        in_specs=[pl.BlockSpec(memory_space=pltpu.SMEM), left_spec, left_spec] + rows_specs * 2,
        out_specs=[out_spec, out_spec],
        out_shape=[jax.ShapeDtypeStruct((rank, width), jnp.bfloat16)] * 2,
        compiler_params=pltpu.CompilerParams(vmem_limit_bytes=VMEM_LIMIT),
        cost_estimate=pl.CostEstimate(
            flops=12 * slots * width * rank, bytes_accessed=4 * width * (slots + rank), transcendentals=0
        ),
    )(factor, left_a, left_b, *blocks_x, *blocks_dy)


def clip_factor(local_sq, adapters, rank, width):
    total = total_over_blk(local_sq[:1, :1])
    mean_sq = total / (2.0 * adapters * rank * width)
    return jnp.minimum(1.0, 1.0 / jnp.sqrt(mean_sq + EPS))


def permute(value, pairs):
    return lax.ppermute(value, "blk", pairs)


def gathered(weight, me):
    lines = [(z, rest) for z in range(4) for rest in range(4)]
    hop = lambda ends: [(z * 4 + rest, ends[z] * 4 + rest) for z, rest in lines if z in ends]
    near = permute(weight, hop({0: 1, 1: 0, 2: 3, 3: 2}))
    across = permute(weight, hop({1: 2, 2: 1}))
    across_near = permute(near, hop({1: 2, 2: 1}))
    outward = permute(across, hop({1: 0, 2: 3}))
    outward_near = permute(across_near, hop({1: 0, 2: 3}))
    plane = me // 4
    inner = (plane == 1) | (plane == 2)
    second = jnp.where(inner, across, outward)
    third = jnp.where(inner, across_near, outward_near)
    pieces = [weight, near, second, third]
    partners = [0, 4, jnp.where(inner, 12, 8), jnp.where(inner, 8, 12)]
    for bit in (2, 1):
        pieces += [permute(piece, [(i, i ^ bit) for i in range(16)]) for piece in pieces]
        partners += [partner + bit for partner in partners]
    return pieces, jnp.stack([jnp.asarray(partner, jnp.int32) for partner in partners])


def per_device_blocks(tokens, cotangent, tenant, owner, down_factor_table, up_factor_table):
    rows, width = tokens.shape
    count_blk = lax.axis_size("blk")
    adapters = owner.shape[0]
    rank = down_factor_table.shape[1]
    cap = 2 * rows // adapters
    down_weight = down_factor_table[0]
    up_weight = up_factor_table[0]
    me = lax.axis_index("blk").astype(jnp.int32)
    order = [8, 1, 9, 2, 10, 3, 11, 4, 12, 5, 13, 6, 14, 7, 15]
    first, second = order[:8], order[8:]

    def swap(value, partner):
        return permute(value, [(i, i ^ partner) for i in range(count_blk)])

    with jax.named_scope("down_factors"):
        pieces, partners = gathered(down_weight, me)
    with jax.named_scope("send_cotangent"):
        own_dy, *sent_dy = place([0] + order, cap, me, owner, tenant, cotangent)
        got_dy = [swap(block, partner) for block, partner in zip(sent_dy, order)]
    with jax.named_scope("grad_hidden_first"):
        low_first = low_products(got_dy[:8], up_weight, SCALE)
    with jax.named_scope("send_tokens_first"):
        sent_first = place(first, cap, me, owner, tenant, tokens, low_first)
        got_x = [swap(block, partner) for block, partner in zip(sent_first, first)]
    with jax.named_scope("grad_hidden"):
        blocks_dy = got_dy + [own_dy]
        grad_hidden, gram_dy = rows_products(blocks_dy, up_weight, SCALE)
    with jax.named_scope("send_tokens_second"):
        *sent_second, own_x = place(second + [0], cap, me, owner, tenant, tokens, grad_hidden[8 * cap :])
        got_x += [swap(block, partner) for block, partner in zip(sent_second, second)]
    with jax.named_scope("hidden"):
        blocks_x = got_x + [own_x]
        hidden, gram_x, extra = rows_products(blocks_x, down_weight, 1.0, with_extra=True)
    with jax.named_scope("fold"):
        amount = jnp.sum(extra[:, rank], dtype=jnp.float32).reshape(1, 1)
        left_a, left_b, local_sq = fold(amount, grad_hidden, gram_x, hidden, gram_dy)
    with jax.named_scope("clip"):
        factor = clip_factor(local_sq, adapters, rank, width)
    with jax.named_scope("grads"):
        grad_a, grad_b = grads(factor, left_a, left_b, blocks_x, blocks_dy, width)
    with jax.named_scope("input_grad"):
        by_partner = dict(zip(order + [0], range(count_blk)))
        extra = jnp.concatenate(
            [extra[by_partner[s] * cap : (by_partner[s] + 1) * cap] for s in range(count_blk)], axis=0
        )
        input_grad = input_grad_of(cap, me, owner, tenant, partners, extra, pieces)
    return (input_grad, grad_a[None], grad_b[None])


def per_device(tokens, cotangent, tenant, owner, down_factor_table, up_factor_table):
    rows, width = tokens.shape
    count_blk = lax.axis_size("blk")
    adapters = owner.shape[0]
    rank = down_factor_table.shape[1]
    cap = 2 * rows // adapters
    slots = count_blk * cap
    down_weight = down_factor_table[0]
    up_weight = up_factor_table[0]

    with jax.named_scope("targets"):
        tenant_ids = tenant[:, 0]
        match = tenant_ids[:, None] == jnp.arange(adapters, dtype=jnp.int32)[None, :]
        target_dev = jnp.sum(jnp.where(match, owner[None, :], 0), axis=1)
        row_ids = jnp.arange(rows, dtype=jnp.int32)
        same_before = (tenant_ids[:, None] == tenant_ids[None, :]) & (row_ids[None, :] < row_ids[:, None])
        position = jnp.sum(same_before.astype(jnp.int32), axis=1)
        target = target_dev * cap + position
        placing = (jnp.arange(slots, dtype=jnp.int32)[:, None] == target[None, :]).astype(jnp.bfloat16)

    def exchange(value):
        value = value.reshape(count_blk, cap, width)
        return lax.all_to_all(value, "blk", split_axis=0, concat_axis=0, tiled=True).reshape(slots, width)

    def place(value):
        return jnp.dot(placing, value, preferred_element_type=jnp.float32).astype(jnp.bfloat16)

    with jax.named_scope("send_cotangent"):
        rows_dy = exchange(place(cotangent))
    with jax.named_scope("send_tokens"):
        rows_x = exchange(place(tokens))
    with jax.named_scope("row_counts"):
        devices = jnp.arange(count_blk, dtype=jnp.int32)
        sent = jnp.sum((target_dev[:, None] == devices[None, :]).astype(jnp.float32), axis=0, keepdims=True)
        counts = total_over_blk(sent)
        amount = jnp.sum(jnp.where(devices == lax.axis_index("blk"), counts[0], 0.0)).reshape(1, 1)
    with jax.named_scope("grad_hidden"):
        grad_hidden, gram_dy = rows_products([rows_dy], up_weight, SCALE)
    with jax.named_scope("back"):
        back = jnp.dot(grad_hidden, down_weight, preferred_element_type=jnp.float32).astype(jnp.bfloat16)
        returned = exchange(back)
    with jax.named_scope("hidden"):
        hidden, gram_x = rows_products([rows_x], down_weight, 1.0)
    with jax.named_scope("fold"):
        left_a, left_b, local_sq = fold(amount, grad_hidden, gram_x, hidden, gram_dy)
    with jax.named_scope("clip"):
        factor = clip_factor(local_sq, adapters, rank, width)
    with jax.named_scope("grads"):
        grad_a, grad_b = grads(factor, left_a, left_b, [rows_x], [rows_dy], width)
    with jax.named_scope("input_grad"):
        input_grad = lax.dot_general(placing, returned, FIRST, preferred_element_type=jnp.float32).astype(
            jnp.bfloat16
        )
    return (input_grad, grad_a[None], grad_b[None])


def solution(mesh):
    body = per_device_blocks if mesh.shape["blk"] == 16 else per_device
    split = ("groups", "blk")
    in_specs = (P(split, None), P(split, None), P(split, None), P("groups"), P(split, None, None), P(split, None, None))
    out_specs = (P(split, None), P(split, None, None), P(split, None, None))
    return jax.shard_map(body, mesh=mesh, in_specs=in_specs, out_specs=out_specs, check_vma=False)
```

```python
import jax
import jax.numpy as jnp
from jax import lax
from jax.experimental import pallas as pl
from jax.experimental.pallas import tpu as pltpu
from jax.sharding import PartitionSpec as P

SCALE = 2.0
DAMPING = 1.0
EPS = 1e-06
VMEM_LIMIT = 48 * 1024 * 1024
LANES = 128
WINDOW = 5
LAST = (((1,), (1,)), ((), ()))
FIRST = (((0,), (0,)), ((), ()))


def total_over_blk(value):
    size = lax.axis_size("blk")
    if size & (size - 1):
        return lax.psum(value, "blk")
    step = 1
    while step < size:
        value = value + lax.ppermute(value, "blk", [(i, i ^ step) for i in range(size)])
        step *= 2
    return value


def rows_kernel(scale, count, with_extra, *refs):
    blocks, extras = refs[:count], refs[count : 2 * count if with_extra else count]
    weight_ref, low_ref, gram_ref, *rest = refs[count + len(extras) :]
    low_total = rest[-1]
    step = pl.program_id(0)

    @pl.when(step == 0)
    def _():
        low_total[...] = jnp.zeros_like(low_total)
        gram_ref[...] = jnp.zeros_like(gram_ref)
        if with_extra:
            rest[0][...] = jnp.concatenate([ref[...] for ref in extras], axis=0)

    rows = jnp.concatenate([ref[...] for ref in blocks], axis=0)
    low_total[...] += lax.dot_general(rows, weight_ref[...], LAST, preferred_element_type=jnp.float32)
    gram_ref[...] += lax.dot_general(rows, rows, LAST, preferred_element_type=jnp.float32)

    @pl.when(step == pl.num_programs(0) - 1)
    def _():
        low_ref[...] = (scale * low_total[...]).astype(low_ref.dtype)


def rows_products(blocks, weight, scale, with_extra=False):
    slots = sum(block.shape[0] for block in blocks)
    rank, width = weight.shape
    chunk = min(width, 2048)
    in_specs = [pl.BlockSpec((block.shape[0], chunk), lambda i: (0, i)) for block in blocks]
    out_specs = [pl.BlockSpec((slots, rank), lambda i: (0, 0)), pl.BlockSpec((slots, slots), lambda i: (0, 0))]
    out_shape = [
        jax.ShapeDtypeStruct((slots, rank), jnp.bfloat16),
        jax.ShapeDtypeStruct((slots, slots), jnp.float32),
    ]
    operands = list(blocks)
    if with_extra:
        in_specs += [
            pl.BlockSpec((block.shape[0], LANES), lambda i, at=block.shape[1] // LANES - 1: (0, at)) for block in blocks
        ]
        operands += list(blocks)
        out_specs.append(pl.BlockSpec((slots, LANES), lambda i: (0, 0)))
        out_shape.append(jax.ShapeDtypeStruct((slots, LANES), jnp.bfloat16))
    return pl.pallas_call(
        lambda *refs: rows_kernel(scale, len(blocks), with_extra, *refs),
        grid=(width // chunk,),
        in_specs=in_specs + [pl.BlockSpec((rank, chunk), lambda i: (0, i))],
        out_specs=out_specs,
        out_shape=out_shape,
        scratch_shapes=[pltpu.VMEM((slots, rank), jnp.float32)],
        compiler_params=pltpu.CompilerParams(vmem_limit_bytes=VMEM_LIMIT),
        cost_estimate=pl.CostEstimate(
            flops=2 * slots * width * (slots + rank),
            bytes_accessed=2 * width * (slots + rank),
            transcendentals=0,
        ),
    )(*operands, weight)


def slot_targets(cap, me, owner_ref, column_ref, row_ref):
    column, row = column_ref[...], row_ref[...]
    rows, adapters = row.shape[1], owner_ref.shape[0]
    adapter = lax.broadcasted_iota(jnp.int32, (adapters, rows), 0)
    device = jnp.sum(jnp.where(adapter == row, owner_ref[...], 0), axis=0, keepdims=True)
    earlier = lax.broadcasted_iota(jnp.int32, (rows, rows), 0) < lax.broadcasted_iota(jnp.int32, (rows, rows), 1)
    position = jnp.sum(jnp.where((column == row) & earlier, 1, 0), axis=0, keepdims=True)
    partner = device ^ me
    return partner, partner * cap + position


def place_kernel(partners, cap, with_live, me_ref, owner_ref, column_ref, row_ref, values_ref, *refs):
    placing = refs[-1]
    low_refs, outs = refs[: len(refs) - 1 - len(partners)], refs[len(refs) - 1 - len(partners) : -1]
    step = pl.program_id(0)
    rows, chunk = row_ref.shape[1], values_ref.shape[1]

    @pl.when(step == 0)
    def _():
        _, target = slot_targets(cap, me_ref[0, 0], owner_ref, column_ref, row_ref)
        slot = lax.broadcasted_iota(jnp.int32, (cap, rows), 0)
        for at, partner in enumerate(partners):
            placing[at * cap : (at + 1) * cap, :] = jnp.where(slot + partner * cap == target, 1.0, 0.0).astype(
                placing.dtype
            )

    placed = jnp.dot(placing[...], values_ref[...], preferred_element_type=jnp.float32).astype(jnp.bfloat16)
    for at, out in enumerate(outs):
        if with_live:
            out[:, pl.ds(pl.multiple_of(step * chunk, chunk), chunk)] = placed[at * cap : (at + 1) * cap]
        else:
            out[...] = placed[at * cap : (at + 1) * cap]

    if with_live:

        @pl.when(step == pl.num_programs(0) - 1)
        def _():
            live = jnp.sum(placing[...].astype(jnp.float32), axis=1, keepdims=True).astype(jnp.bfloat16)
            for at, out in enumerate(outs):
                full = out.shape[1]
                out[:, full - LANES :] = jnp.broadcast_to(live[at * cap : (at + 1) * cap], (cap, LANES))
                if low_refs:
                    low = low_refs[0][...].astype(jnp.float32)
                    lanes = [low[q * cap : (q + 1) * cap] for q in range(low.shape[0] // cap)]
                    out[:, pl.num_programs(0) * chunk : full - LANES] = jnp.concatenate(lanes, axis=1).astype(
                        jnp.bfloat16
                    )


def place(partners, cap, me, owner, tenant, values, with_live=False, low=None):
    rows, width = values.shape
    adapters = owner.shape[0]
    full = width + (LANES if with_live else 0) + (low.size // cap if low is not None else 0)
    chunk = min(width, 2048)
    still = lambda shape: pl.BlockSpec(shape, lambda i: (0, 0))
    in_specs = [
        pl.BlockSpec(memory_space=pltpu.SMEM),
        still((adapters, 1)),
        still((rows, 1)),
        still((1, rows)),
        pl.BlockSpec((rows, chunk), lambda i: (0, i)),
    ]
    operands = [me.reshape(1, 1), owner.reshape(adapters, 1), tenant, tenant.reshape(1, rows), values]
    if low is not None:
        in_specs.append(still(low.shape))
        operands.append(low)
    out_spec = still((cap, full)) if with_live else pl.BlockSpec((cap, chunk), lambda i: (0, i))
    return pl.pallas_call(
        lambda *refs: place_kernel(partners, cap, with_live, *refs),
        grid=(width // chunk,),
        in_specs=in_specs,
        out_specs=[out_spec] * len(partners),
        out_shape=[jax.ShapeDtypeStruct((cap, full), jnp.bfloat16)] * len(partners),
        scratch_shapes=[pltpu.VMEM((len(partners) * cap, rows), jnp.bfloat16)],
        compiler_params=pltpu.CompilerParams(vmem_limit_bytes=VMEM_LIMIT),
        cost_estimate=pl.CostEstimate(
            flops=2 * len(partners) * cap * rows * width,
            bytes_accessed=2 * width * (rows + len(partners) * cap),
            transcendentals=0,
        ),
    )(*operands)


def back_kernel(count, stacked, low_ref, weight_ref, *outs):
    cap = outs[0].shape[0]
    rank = weight_ref.shape[0]
    if stacked:
        low = low_ref[...].astype(jnp.float32)
        low = jnp.concatenate([low[:, at * rank : (at + 1) * rank] for at in range(count)], axis=0)
        low = low.astype(jnp.bfloat16)
    else:
        low = low_ref[...]
    rows = jnp.dot(low, weight_ref[...], preferred_element_type=jnp.float32).astype(jnp.bfloat16)
    for at, out in enumerate(outs):
        out[...] = rows[at * cap : (at + 1) * cap]


def back_rows(count, cap, low, weight, low_spec, stacked):
    rank, width = weight.shape
    chunk = min(width, 2048)
    return pl.pallas_call(
        lambda *refs: back_kernel(count, stacked, *refs),
        grid=(width // chunk,),
        in_specs=[low_spec, pl.BlockSpec((rank, chunk), lambda i: (0, i))],
        out_specs=[pl.BlockSpec((cap, chunk), lambda i: (0, i))] * count,
        out_shape=[jax.ShapeDtypeStruct((cap, width), jnp.bfloat16)] * count,
        compiler_params=pltpu.CompilerParams(vmem_limit_bytes=VMEM_LIMIT),
        cost_estimate=pl.CostEstimate(
            flops=2 * count * cap * rank * width, bytes_accessed=2 * width * (rank + count * cap), transcendentals=0
        ),
    )(low, weight)


def input_grad_kernel(cap, count, me_ref, owner_ref, column_ref, row_ref, *refs):
    blocks, out_ref, placing = refs[:count], refs[count], refs[count + 1]
    step = pl.program_id(0)

    @pl.when(step == 0)
    def _():
        _, target = slot_targets(cap, me_ref[0, 0], owner_ref, column_ref, row_ref)
        slot = lax.broadcasted_iota(jnp.int32, placing.shape, 0)
        placing[...] = jnp.where(slot == target, 1.0, 0.0).astype(placing.dtype)

    returned = jnp.concatenate([ref[...] for ref in blocks], axis=0)
    out_ref[...] = lax.dot_general(placing[...], returned, FIRST, preferred_element_type=jnp.float32).astype(
        out_ref.dtype
    )


def input_grad_of(cap, me, owner, tenant, blocks):
    rows, adapters, count = tenant.shape[0], owner.shape[0], len(blocks)
    width = blocks[0].shape[1]
    chunk = min(width, 2048)
    still = lambda shape: pl.BlockSpec(shape, lambda i: (0, 0))
    return pl.pallas_call(
        lambda *refs: input_grad_kernel(cap, count, *refs),
        grid=(width // chunk,),
        in_specs=[
            pl.BlockSpec(memory_space=pltpu.SMEM),
            still((adapters, 1)),
            still((rows, 1)),
            still((1, rows)),
        ]
        + [pl.BlockSpec((cap, chunk), lambda i: (0, i))] * count,
        out_specs=pl.BlockSpec((rows, chunk), lambda i: (0, i)),
        out_shape=jax.ShapeDtypeStruct((rows, width), jnp.bfloat16),
        scratch_shapes=[pltpu.VMEM((count * cap, rows), jnp.bfloat16)],
        compiler_params=pltpu.CompilerParams(vmem_limit_bytes=VMEM_LIMIT),
        cost_estimate=pl.CostEstimate(
            flops=2 * rows * count * cap * width,
            bytes_accessed=2 * width * (rows + count * cap),
            transcendentals=0,
        ),
    )(me.reshape(1, 1), owner.reshape(adapters, 1), tenant, tenant.reshape(1, rows), *blocks)


def fold_one(low, gram, scale, amount):
    high = lax.Precision.HIGHEST
    low = low.astype(jnp.float32)
    slots = low.shape[0]
    left = jnp.sum(low, axis=0, keepdims=True) / amount
    raw = scale * low
    along = jnp.sum(raw * left, axis=1, keepdims=True)
    inner = raw - along * left / (DAMPING + jnp.sum(left * left))
    cross = jnp.sum(gram, axis=1, keepdims=True) / amount
    right_sq = jnp.sum(cross) / amount
    side = jnp.sum(inner * cross, axis=0, keepdims=True)
    factor = inner - side / (amount * (DAMPING + right_sq))
    spread = jnp.dot(gram, factor, precision=high, preferred_element_type=jnp.float32)
    return factor, jnp.sum(spread * factor)


def split3(value):
    first = value.astype(jnp.bfloat16)
    rest = value - first.astype(jnp.float32)
    second = rest.astype(jnp.bfloat16)
    third = (rest - second.astype(jnp.float32)).astype(jnp.bfloat16)
    return first, second, third


def fold_kernel(amount_ref, gh_ref, gram_x_ref, hidden_ref, gram_dy_ref, left_a_ref, left_b_ref, sq_ref):
    amount = amount_ref[0, 0]
    rank = gh_ref.shape[1]
    factor_a, sq_a = fold_one(gh_ref[...], gram_x_ref[...], 1.0, amount)
    factor_b, sq_b = fold_one(hidden_ref[...], gram_dy_ref[...], SCALE, amount)
    for out_ref, factor in ((left_a_ref, factor_a), (left_b_ref, factor_b)):
        for at, part in enumerate(split3(factor)):
            out_ref[:, at * rank : (at + 1) * rank] = part
    sq_ref[...] = jnp.zeros_like(sq_ref) + (sq_a + sq_b)


def fold(amount, grad_hidden, gram_x, hidden, gram_dy):
    slots, rank = hidden.shape
    whole = lambda shape: pl.BlockSpec(shape, lambda: (0, 0))
    return pl.pallas_call(
        fold_kernel,
        in_specs=[pl.BlockSpec(memory_space=pltpu.SMEM)]
        + [whole((slots, rank)), whole((slots, slots))] * 2,
        out_specs=[whole((slots, 3 * rank))] * 2 + [whole((8, 128))],
        out_shape=[jax.ShapeDtypeStruct((slots, 3 * rank), jnp.bfloat16)] * 2
        + [jax.ShapeDtypeStruct((8, 128), jnp.float32)],
        compiler_params=pltpu.CompilerParams(vmem_limit_bytes=VMEM_LIMIT),
        cost_estimate=pl.CostEstimate(
            flops=24 * slots * slots * rank, bytes_accessed=12 * slots * slots, transcendentals=0
        ),
    )(amount, grad_hidden, gram_x, hidden, gram_dy)


def grads_kernel(count, factor_ref, left_a_ref, left_b_ref, *refs):
    blocks_x, blocks_dy = refs[:count], refs[count : 2 * count]
    grad_a_ref, grad_b_ref = refs[2 * count :]
    factor = factor_ref[0, 0]
    rank = grad_a_ref.shape[0]
    for left_ref, blocks, out_ref in ((left_a_ref, blocks_x, grad_a_ref), (left_b_ref, blocks_dy, grad_b_ref)):
        rows = jnp.concatenate([ref[...] for ref in blocks], axis=0)
        parts = lax.dot_general(left_ref[...], rows, FIRST, preferred_element_type=jnp.float32)
        proj = (parts[2 * rank :] + parts[rank : 2 * rank]) + parts[:rank]
        out_ref[...] = (factor * proj).astype(out_ref.dtype)


def grads(factor, left_a, left_b, blocks_x, blocks_dy, width):
    slots = left_a.shape[0]
    rank = left_a.shape[1] // 3
    chunk = min(width, 2048)
    left_spec = pl.BlockSpec((slots, 3 * rank), lambda i: (0, 0))
    rows_specs = [pl.BlockSpec((block.shape[0], chunk), lambda i: (0, i)) for block in blocks_x]
    out_spec = pl.BlockSpec((rank, chunk), lambda i: (0, i))
    return pl.pallas_call(
        lambda *refs: grads_kernel(len(blocks_x), *refs),
        grid=(width // chunk,),
        in_specs=[pl.BlockSpec(memory_space=pltpu.SMEM), left_spec, left_spec] + rows_specs * 2,
        out_specs=[out_spec, out_spec],
        out_shape=[jax.ShapeDtypeStruct((rank, width), jnp.bfloat16)] * 2,
        compiler_params=pltpu.CompilerParams(vmem_limit_bytes=VMEM_LIMIT),
        cost_estimate=pl.CostEstimate(
            flops=12 * slots * width * rank, bytes_accessed=4 * width * (slots + rank), transcendentals=0
        ),
    )(factor, left_a, left_b, *blocks_x, *blocks_dy)


def clip_factor(local_sq, adapters, rank, width):
    total = total_over_blk(local_sq[:1, :1])
    mean_sq = total / (2.0 * adapters * rank * width)
    return jnp.minimum(1.0, 1.0 / jnp.sqrt(mean_sq + EPS))


class Line:
    def __init__(self, window):
        self.window = window
        self.results = []

    def swap(self, value, partner):
        if len(self.results) >= self.window:
            value, _ = lax.optimization_barrier((value, self.results[-self.window]))
        size = lax.axis_size("blk")
        result = lax.ppermute(value, "blk", [(i, i ^ partner) for i in range(size)])
        self.results.append(result)
        return result


def per_device_blocks(tokens, cotangent, tenant, owner, down_factor_table, up_factor_table):
    rows, width = tokens.shape
    count_blk = lax.axis_size("blk")
    half = count_blk // 2
    adapters = owner.shape[0]
    rank = down_factor_table.shape[1]
    cap = 2 * rows // adapters
    down_weight = down_factor_table[0]
    up_weight = up_factor_table[0]
    me = lax.axis_index("blk").astype(jnp.int32)
    line = Line(WINDOW)
    low_of = lambda low, first, count: low[first * cap : (first + count) * cap]

    order = [half]
    for s in range(1, half):
        order += [s, half + s]
    sent_dy = place(list(range(count_blk)), cap, me, owner, tenant, cotangent)
    got_dy = {0: sent_dy[0]}
    for s in order:
        got_dy[s] = line.swap(sent_dy[s], s)

    others = [s for s in range(count_blk) if s != half]
    sent_x = dict(zip(others, place(others, cap, me, owner, tenant, tokens, with_live=True)))
    got_x = {0: sent_x[0]}
    parts = 4
    mirror_parts = []
    for part in range(parts):
        columns = slice(part * width // parts, (part + 1) * width // parts)
        mirror_parts.append(line.swap(down_weight[:, columns], half))
        got_x[part + 1] = line.swap(sent_x[part + 1], part + 1)

    blocks_dy = [got_dy[s] for s in range(count_blk)]
    grad_hidden, gram_dy = rows_products(blocks_dy, up_weight, SCALE)
    (sent_mirror,) = place(
        [half], cap, me, owner, tenant, tokens, with_live=True, low=low_of(grad_hidden, half, half)
    )
    got_x[half] = line.swap(sent_mirror, half)
    still = pl.BlockSpec((half * cap, rank), lambda i: (0, 0))
    own_back = back_rows(half, cap, low_of(grad_hidden, 0, half), down_weight, still, False)
    back = {0: own_back[0]}
    rest = [s for s in order if s > parts and s != half]
    for at, s in enumerate(rest):
        got_x[s] = line.swap(sent_x[s], s)
        if at % 2 == 1 and len(back) < half:
            back[len(back)] = line.swap(own_back[len(back)], len(back))
    while len(back) < half:
        back[len(back)] = line.swap(own_back[len(back)], len(back))
    mirror_low = pl.BlockSpec((cap, half * rank), lambda i: (0, width // (half * rank)))
    mirror_weight = jnp.concatenate(mirror_parts, axis=1)
    mirror_back = back_rows(half, cap, got_x[half], mirror_weight, mirror_low, True)
    back[half] = mirror_back[0]
    for s in range(1, half):
        back[half + s] = line.swap(mirror_back[s], s)

    blocks_x = [got_x[s] for s in range(count_blk)]
    hidden, gram_x, live = rows_products(blocks_x, down_weight, 1.0, with_extra=True)
    amount = jnp.sum(live[:, 0], dtype=jnp.float32).reshape(1, 1)
    left_a, left_b, local_sq = fold(amount, grad_hidden, gram_x, hidden, gram_dy)
    factor = clip_factor(local_sq, adapters, rank, width)
    grad_a, grad_b = grads(factor, left_a, left_b, blocks_x, blocks_dy, width)
    input_grad = input_grad_of(cap, me, owner, tenant, [back[s] for s in range(count_blk)])
    return (input_grad, grad_a[None], grad_b[None])


def per_device(tokens, cotangent, tenant, owner, down_factor_table, up_factor_table):
    rows, width = tokens.shape
    count_blk = lax.axis_size("blk")
    adapters = owner.shape[0]
    rank = down_factor_table.shape[1]
    cap = 2 * rows // adapters
    slots = count_blk * cap
    down_weight = down_factor_table[0]
    up_weight = up_factor_table[0]

    with jax.named_scope("targets"):
        tenant_ids = tenant[:, 0]
        match = tenant_ids[:, None] == jnp.arange(adapters, dtype=jnp.int32)[None, :]
        target_dev = jnp.sum(jnp.where(match, owner[None, :], 0), axis=1)
        row_ids = jnp.arange(rows, dtype=jnp.int32)
        same_before = (tenant_ids[:, None] == tenant_ids[None, :]) & (row_ids[None, :] < row_ids[:, None])
        position = jnp.sum(same_before.astype(jnp.int32), axis=1)
        target = target_dev * cap + position
        placing = (jnp.arange(slots, dtype=jnp.int32)[:, None] == target[None, :]).astype(jnp.bfloat16)

    def exchange(value):
        value = value.reshape(count_blk, cap, width)
        return lax.all_to_all(value, "blk", split_axis=0, concat_axis=0, tiled=True).reshape(slots, width)

    def place(value):
        return jnp.dot(placing, value, preferred_element_type=jnp.float32).astype(jnp.bfloat16)

    with jax.named_scope("send_cotangent"):
        rows_dy = exchange(place(cotangent))
    with jax.named_scope("send_tokens"):
        rows_x = exchange(place(tokens))
    with jax.named_scope("row_counts"):
        devices = jnp.arange(count_blk, dtype=jnp.int32)
        sent = jnp.sum((target_dev[:, None] == devices[None, :]).astype(jnp.float32), axis=0, keepdims=True)
        counts = total_over_blk(sent)
        amount = jnp.sum(jnp.where(devices == lax.axis_index("blk"), counts[0], 0.0)).reshape(1, 1)
    with jax.named_scope("grad_hidden"):
        grad_hidden, gram_dy = rows_products([rows_dy], up_weight, SCALE)
    with jax.named_scope("back"):
        back = jnp.dot(grad_hidden, down_weight, preferred_element_type=jnp.float32).astype(jnp.bfloat16)
        returned = exchange(back)
    with jax.named_scope("hidden"):
        hidden, gram_x = rows_products([rows_x], down_weight, 1.0)
    with jax.named_scope("fold"):
        left_a, left_b, local_sq = fold(amount, grad_hidden, gram_x, hidden, gram_dy)
    with jax.named_scope("clip"):
        factor = clip_factor(local_sq, adapters, rank, width)
    with jax.named_scope("grads"):
        grad_a, grad_b = grads(factor, left_a, left_b, [rows_x], [rows_dy], width)
    with jax.named_scope("input_grad"):
        input_grad = lax.dot_general(placing, returned, FIRST, preferred_element_type=jnp.float32).astype(
            jnp.bfloat16
        )
    return (input_grad, grad_a[None], grad_b[None])


def solution(mesh):
    body = per_device_blocks if mesh.shape["blk"] == 16 else per_device
    split = ("groups", "blk")
    in_specs = (P(split, None), P(split, None), P(split, None), P("groups"), P(split, None, None), P(split, None, None))
    out_specs = (P(split, None), P(split, None, None), P(split, None, None))
    return jax.shard_map(body, mesh=mesh, in_specs=in_specs, out_specs=out_specs, check_vma=False)
```

```python
import jax
import jax.numpy as jnp
from jax import lax
from jax.experimental import pallas as pl
from jax.experimental.pallas import tpu as pltpu
from jax.sharding import PartitionSpec as P

SCALE = 2.0
DAMPING = 1.0
EPS = 1e-06
VMEM_LIMIT = 48 * 1024 * 1024
LANES = 128
FAR_WINDOW = 4
NEAR_WINDOW = 4
LAST = (((1,), (1,)), ((), ()))
FIRST = (((0,), (0,)), ((), ()))


def total_over_blk(value):
    size = lax.axis_size("blk")
    if size & (size - 1):
        return lax.psum(value, "blk")
    step = 1
    while step < size:
        value = value + lax.ppermute(value, "blk", [(i, i ^ step) for i in range(size)])
        step *= 2
    return value


def rows_kernel(scale, count, with_extra, *refs):
    blocks, extras = refs[:count], refs[count : 2 * count if with_extra else count]
    weight_ref, low_ref, gram_ref, *rest = refs[count + len(extras) :]
    low_total = rest[-1]
    step = pl.program_id(0)

    @pl.when(step == 0)
    def _():
        low_total[...] = jnp.zeros_like(low_total)
        gram_ref[...] = jnp.zeros_like(gram_ref)
        if with_extra:
            rest[0][...] = jnp.concatenate([ref[...] for ref in extras], axis=0)

    rows = jnp.concatenate([ref[...] for ref in blocks], axis=0)
    low_total[...] += lax.dot_general(rows, weight_ref[...], LAST, preferred_element_type=jnp.float32)
    gram_ref[...] += lax.dot_general(rows, rows, LAST, preferred_element_type=jnp.float32)

    @pl.when(step == pl.num_programs(0) - 1)
    def _():
        low_ref[...] = (scale * low_total[...]).astype(low_ref.dtype)


def rows_products(blocks, weight, scale, with_extra=False):
    slots = sum(block.shape[0] for block in blocks)
    rank, width = weight.shape
    chunk = min(width, 2048)
    in_specs = [pl.BlockSpec((block.shape[0], chunk), lambda i: (0, i)) for block in blocks]
    out_specs = [pl.BlockSpec((slots, rank), lambda i: (0, 0)), pl.BlockSpec((slots, slots), lambda i: (0, 0))]
    out_shape = [
        jax.ShapeDtypeStruct((slots, rank), jnp.bfloat16),
        jax.ShapeDtypeStruct((slots, slots), jnp.float32),
    ]
    operands = list(blocks)
    if with_extra:
        in_specs += [
            pl.BlockSpec((block.shape[0], LANES), lambda i, at=block.shape[1] // LANES - 1: (0, at)) for block in blocks
        ]
        operands += list(blocks)
        out_specs.append(pl.BlockSpec((slots, LANES), lambda i: (0, 0)))
        out_shape.append(jax.ShapeDtypeStruct((slots, LANES), jnp.bfloat16))
    return pl.pallas_call(
        lambda *refs: rows_kernel(scale, len(blocks), with_extra, *refs),
        grid=(width // chunk,),
        in_specs=in_specs + [pl.BlockSpec((rank, chunk), lambda i: (0, i))],
        out_specs=out_specs,
        out_shape=out_shape,
        scratch_shapes=[pltpu.VMEM((slots, rank), jnp.float32)],
        compiler_params=pltpu.CompilerParams(vmem_limit_bytes=VMEM_LIMIT),
        cost_estimate=pl.CostEstimate(
            flops=2 * slots * width * (slots + rank),
            bytes_accessed=2 * width * (slots + rank),
            transcendentals=0,
        ),
    )(*operands, weight)


def slot_targets(cap, me, owner_ref, column_ref, row_ref):
    column, row = column_ref[...], row_ref[...]
    rows, adapters = row.shape[1], owner_ref.shape[0]
    adapter = lax.broadcasted_iota(jnp.int32, (adapters, rows), 0)
    device = jnp.sum(jnp.where(adapter == row, owner_ref[...], 0), axis=0, keepdims=True)
    earlier = lax.broadcasted_iota(jnp.int32, (rows, rows), 0) < lax.broadcasted_iota(jnp.int32, (rows, rows), 1)
    position = jnp.sum(jnp.where((column == row) & earlier, 1, 0), axis=0, keepdims=True)
    partner = device ^ me
    return partner, partner * cap + position


def place_kernel(partners, cap, with_live, me_ref, owner_ref, column_ref, row_ref, values_ref, *refs):
    placing = refs[-1]
    low_refs, outs = refs[: len(refs) - 1 - len(partners)], refs[len(refs) - 1 - len(partners) : -1]
    step = pl.program_id(0)
    rows, chunk = row_ref.shape[1], values_ref.shape[1]

    @pl.when(step == 0)
    def _():
        _, target = slot_targets(cap, me_ref[0, 0], owner_ref, column_ref, row_ref)
        slot = lax.broadcasted_iota(jnp.int32, (cap, rows), 0)
        for at, partner in enumerate(partners):
            placing[at * cap : (at + 1) * cap, :] = jnp.where(slot + partner * cap == target, 1.0, 0.0).astype(
                placing.dtype
            )

    placed = jnp.dot(placing[...], values_ref[...], preferred_element_type=jnp.float32).astype(jnp.bfloat16)
    for at, out in enumerate(outs):
        if with_live:
            out[:, pl.ds(pl.multiple_of(step * chunk, chunk), chunk)] = placed[at * cap : (at + 1) * cap]
        else:
            out[...] = placed[at * cap : (at + 1) * cap]

    if with_live:

        @pl.when(step == pl.num_programs(0) - 1)
        def _():
            live = jnp.sum(placing[...].astype(jnp.float32), axis=1, keepdims=True).astype(jnp.bfloat16)
            for at, out in enumerate(outs):
                full = out.shape[1]
                out[:, full - LANES :] = jnp.broadcast_to(live[at * cap : (at + 1) * cap], (cap, LANES))
                if low_refs:
                    low = low_refs[0][...].astype(jnp.float32)
                    lanes = [low[q * cap : (q + 1) * cap] for q in range(low.shape[0] // cap)]
                    out[:, pl.num_programs(0) * chunk : full - LANES] = jnp.concatenate(lanes, axis=1).astype(
                        jnp.bfloat16
                    )


def place(partners, cap, me, owner, tenant, values, with_live=False, low=None):
    rows, width = values.shape
    adapters = owner.shape[0]
    full = width + (LANES if with_live else 0) + (low.size // cap if low is not None else 0)
    chunk = min(width, 2048)
    still = lambda shape: pl.BlockSpec(shape, lambda i: (0, 0))
    in_specs = [
        pl.BlockSpec(memory_space=pltpu.SMEM),
        still((adapters, 1)),
        still((rows, 1)),
        still((1, rows)),
        pl.BlockSpec((rows, chunk), lambda i: (0, i)),
    ]
    operands = [me.reshape(1, 1), owner.reshape(adapters, 1), tenant, tenant.reshape(1, rows), values]
    if low is not None:
        in_specs.append(still(low.shape))
        operands.append(low)
    out_spec = still((cap, full)) if with_live else pl.BlockSpec((cap, chunk), lambda i: (0, i))
    return pl.pallas_call(
        lambda *refs: place_kernel(partners, cap, with_live, *refs),
        grid=(width // chunk,),
        in_specs=in_specs,
        out_specs=[out_spec] * len(partners),
        out_shape=[jax.ShapeDtypeStruct((cap, full), jnp.bfloat16)] * len(partners),
        scratch_shapes=[pltpu.VMEM((len(partners) * cap, rows), jnp.bfloat16)],
        compiler_params=pltpu.CompilerParams(vmem_limit_bytes=VMEM_LIMIT),
        cost_estimate=pl.CostEstimate(
            flops=2 * len(partners) * cap * rows * width,
            bytes_accessed=2 * width * (rows + len(partners) * cap),
            transcendentals=0,
        ),
    )(*operands)


def back_kernel(count, stacked, low_ref, weight_ref, *outs):
    cap = outs[0].shape[0]
    rank = weight_ref.shape[0]
    if stacked:
        low = low_ref[...].astype(jnp.float32)
        low = jnp.concatenate([low[:, at * rank : (at + 1) * rank] for at in range(count)], axis=0)
        low = low.astype(jnp.bfloat16)
    else:
        low = low_ref[...]
    rows = jnp.dot(low, weight_ref[...], preferred_element_type=jnp.float32).astype(jnp.bfloat16)
    for at, out in enumerate(outs):
        out[...] = rows[at * cap : (at + 1) * cap]


def back_rows(count, cap, low, weight, low_spec, stacked):
    rank, width = weight.shape
    chunk = min(width, 2048)
    return pl.pallas_call(
        lambda *refs: back_kernel(count, stacked, *refs),
        grid=(width // chunk,),
        in_specs=[low_spec, pl.BlockSpec((rank, chunk), lambda i: (0, i))],
        out_specs=[pl.BlockSpec((cap, chunk), lambda i: (0, i))] * count,
        out_shape=[jax.ShapeDtypeStruct((cap, width), jnp.bfloat16)] * count,
        compiler_params=pltpu.CompilerParams(vmem_limit_bytes=VMEM_LIMIT),
        cost_estimate=pl.CostEstimate(
            flops=2 * count * cap * rank * width, bytes_accessed=2 * width * (rank + count * cap), transcendentals=0
        ),
    )(low, weight)


def input_grad_kernel(cap, count, me_ref, owner_ref, column_ref, row_ref, *refs):
    blocks, out_ref, placing = refs[:count], refs[count], refs[count + 1]
    step = pl.program_id(0)

    @pl.when(step == 0)
    def _():
        _, target = slot_targets(cap, me_ref[0, 0], owner_ref, column_ref, row_ref)
        slot = lax.broadcasted_iota(jnp.int32, placing.shape, 0)
        placing[...] = jnp.where(slot == target, 1.0, 0.0).astype(placing.dtype)

    returned = jnp.concatenate([ref[...] for ref in blocks], axis=0)
    out_ref[...] = lax.dot_general(placing[...], returned, FIRST, preferred_element_type=jnp.float32).astype(
        out_ref.dtype
    )


def input_grad_of(cap, me, owner, tenant, blocks):
    rows, adapters, count = tenant.shape[0], owner.shape[0], len(blocks)
    width = blocks[0].shape[1]
    chunk = min(width, 2048)
    still = lambda shape: pl.BlockSpec(shape, lambda i: (0, 0))
    return pl.pallas_call(
        lambda *refs: input_grad_kernel(cap, count, *refs),
        grid=(width // chunk,),
        in_specs=[
            pl.BlockSpec(memory_space=pltpu.SMEM),
            still((adapters, 1)),
            still((rows, 1)),
            still((1, rows)),
        ]
        + [pl.BlockSpec((cap, chunk), lambda i: (0, i))] * count,
        out_specs=pl.BlockSpec((rows, chunk), lambda i: (0, i)),
        out_shape=jax.ShapeDtypeStruct((rows, width), jnp.bfloat16),
        scratch_shapes=[pltpu.VMEM((count * cap, rows), jnp.bfloat16)],
        compiler_params=pltpu.CompilerParams(vmem_limit_bytes=VMEM_LIMIT),
        cost_estimate=pl.CostEstimate(
            flops=2 * rows * count * cap * width,
            bytes_accessed=2 * width * (rows + count * cap),
            transcendentals=0,
        ),
    )(me.reshape(1, 1), owner.reshape(adapters, 1), tenant, tenant.reshape(1, rows), *blocks)


def fold_one(low, gram, scale, amount):
    high = lax.Precision.HIGHEST
    low = low.astype(jnp.float32)
    slots = low.shape[0]
    left = jnp.sum(low, axis=0, keepdims=True) / amount
    raw = scale * low
    along = jnp.sum(raw * left, axis=1, keepdims=True)
    inner = raw - along * left / (DAMPING + jnp.sum(left * left))
    cross = jnp.sum(gram, axis=1, keepdims=True) / amount
    right_sq = jnp.sum(cross) / amount
    side = jnp.sum(inner * cross, axis=0, keepdims=True)
    factor = inner - side / (amount * (DAMPING + right_sq))
    spread = jnp.dot(gram, factor, precision=high, preferred_element_type=jnp.float32)
    return factor, jnp.sum(spread * factor)


def split3(value):
    first = value.astype(jnp.bfloat16)
    rest = value - first.astype(jnp.float32)
    second = rest.astype(jnp.bfloat16)
    third = (rest - second.astype(jnp.float32)).astype(jnp.bfloat16)
    return first, second, third


def fold_kernel(amount_ref, gh_ref, gram_x_ref, hidden_ref, gram_dy_ref, left_a_ref, left_b_ref, sq_ref):
    amount = amount_ref[0, 0]
    rank = gh_ref.shape[1]
    factor_a, sq_a = fold_one(gh_ref[...], gram_x_ref[...], 1.0, amount)
    factor_b, sq_b = fold_one(hidden_ref[...], gram_dy_ref[...], SCALE, amount)
    for out_ref, factor in ((left_a_ref, factor_a), (left_b_ref, factor_b)):
        for at, part in enumerate(split3(factor)):
            out_ref[:, at * rank : (at + 1) * rank] = part
    sq_ref[...] = jnp.zeros_like(sq_ref) + (sq_a + sq_b)


def fold(amount, grad_hidden, gram_x, hidden, gram_dy):
    slots, rank = hidden.shape
    whole = lambda shape: pl.BlockSpec(shape, lambda: (0, 0))
    return pl.pallas_call(
        fold_kernel,
        in_specs=[pl.BlockSpec(memory_space=pltpu.SMEM)]
        + [whole((slots, rank)), whole((slots, slots))] * 2,
        out_specs=[whole((slots, 3 * rank))] * 2 + [whole((8, 128))],
        out_shape=[jax.ShapeDtypeStruct((slots, 3 * rank), jnp.bfloat16)] * 2
        + [jax.ShapeDtypeStruct((8, 128), jnp.float32)],
        compiler_params=pltpu.CompilerParams(vmem_limit_bytes=VMEM_LIMIT),
        cost_estimate=pl.CostEstimate(
            flops=24 * slots * slots * rank, bytes_accessed=12 * slots * slots, transcendentals=0
        ),
    )(amount, grad_hidden, gram_x, hidden, gram_dy)


def grads_kernel(count, factor_ref, left_a_ref, left_b_ref, *refs):
    blocks_x, blocks_dy = refs[:count], refs[count : 2 * count]
    grad_a_ref, grad_b_ref = refs[2 * count :]
    factor = factor_ref[0, 0]
    rank = grad_a_ref.shape[0]
    for left_ref, blocks, out_ref in ((left_a_ref, blocks_x, grad_a_ref), (left_b_ref, blocks_dy, grad_b_ref)):
        rows = jnp.concatenate([ref[...] for ref in blocks], axis=0)
        parts = lax.dot_general(left_ref[...], rows, FIRST, preferred_element_type=jnp.float32)
        proj = (parts[2 * rank :] + parts[rank : 2 * rank]) + parts[:rank]
        out_ref[...] = (factor * proj).astype(out_ref.dtype)


def grads(factor, left_a, left_b, blocks_x, blocks_dy, width):
    slots = left_a.shape[0]
    rank = left_a.shape[1] // 3
    chunk = min(width, 2048)
    left_spec = pl.BlockSpec((slots, 3 * rank), lambda i: (0, 0))
    rows_specs = [pl.BlockSpec((block.shape[0], chunk), lambda i: (0, i)) for block in blocks_x]
    out_spec = pl.BlockSpec((rank, chunk), lambda i: (0, i))
    return pl.pallas_call(
        lambda *refs: grads_kernel(len(blocks_x), *refs),
        grid=(width // chunk,),
        in_specs=[pl.BlockSpec(memory_space=pltpu.SMEM), left_spec, left_spec] + rows_specs * 2,
        out_specs=[out_spec, out_spec],
        out_shape=[jax.ShapeDtypeStruct((rank, width), jnp.bfloat16)] * 2,
        compiler_params=pltpu.CompilerParams(vmem_limit_bytes=VMEM_LIMIT),
        cost_estimate=pl.CostEstimate(
            flops=12 * slots * width * rank, bytes_accessed=4 * width * (slots + rank), transcendentals=0
        ),
    )(factor, left_a, left_b, *blocks_x, *blocks_dy)


def clip_factor(local_sq, adapters, rank, width):
    total = total_over_blk(local_sq[:1, :1])
    mean_sq = total / (2.0 * adapters * rank * width)
    return jnp.minimum(1.0, 1.0 / jnp.sqrt(mean_sq + EPS))


class Line:
    def __init__(self, window):
        self.window = window
        self.results = []

    def swap(self, value, partner):
        if len(self.results) >= self.window:
            value, _ = lax.optimization_barrier((value, self.results[-self.window]))
        size = lax.axis_size("blk")
        result = lax.ppermute(value, "blk", [(i, i ^ partner) for i in range(size)])
        self.results.append(result)
        return result


def per_device_blocks(tokens, cotangent, tenant, owner, down_factor_table, up_factor_table):
    rows, width = tokens.shape
    count_blk = lax.axis_size("blk")
    half = count_blk // 2
    adapters = owner.shape[0]
    rank = down_factor_table.shape[1]
    cap = 2 * rows // adapters
    down_weight = down_factor_table[0]
    up_weight = up_factor_table[0]
    me = lax.axis_index("blk").astype(jnp.int32)
    far, near = Line(FAR_WINDOW), Line(NEAR_WINDOW)
    low_of = lambda low, first, count: low[first * cap : (first + count) * cap]
    parts = rank // cap
    mirror_parts = []

    def send_weight(number):
        for _ in range(number):
            at = len(mirror_parts)
            mirror_parts.append(far.swap(down_weight[at * cap : (at + 1) * cap], half))

    send_weight(parts // 2)
    sent_dy = place(list(range(count_blk)), cap, me, owner, tenant, cotangent)
    others = [s for s in range(count_blk) if s != half]
    sent_x = dict(zip(others, place(others, cap, me, owner, tenant, tokens, with_live=True)))
    got_dy, got_x = {0: sent_dy[0]}, {0: sent_x[0]}
    near_queue = [(got_dy, sent_dy, s) for s in range(1, half)] + [(got_x, sent_x, s) for s in range(1, half)]
    for s in range(half, count_blk):
        got_dy[s] = far.swap(sent_dy[s], s)
        for got, sent, partner in near_queue[:2]:
            got[partner] = near.swap(sent[partner], partner)
        del near_queue[:2]
    send_weight(parts - len(mirror_parts))

    blocks_dy = [got_dy[s] for s in range(count_blk)]
    grad_hidden, gram_dy = rows_products(blocks_dy, up_weight, SCALE)
    (sent_mirror,) = place(
        [half], cap, me, owner, tenant, tokens, with_live=True, low=low_of(grad_hidden, half, half)
    )
    still = pl.BlockSpec((half * cap, rank), lambda i: (0, 0))
    own_back = back_rows(half, cap, low_of(grad_hidden, 0, half), down_weight, still, False)
    back = {0: own_back[0]}
    got_x[half + 1] = far.swap(sent_x[half + 1], half + 1)
    got_x[half] = far.swap(sent_mirror, half)
    for s in range(1, half // 2):
        got_x[half + 1 + s] = far.swap(sent_x[half + 1 + s], half + 1 + s)
        for at in (2 * s - 1, 2 * s):
            back[at] = near.swap(own_back[at], at)
    back[half - 1] = near.swap(own_back[half - 1], half - 1)
    mirror_low = pl.BlockSpec((cap, half * rank), lambda i: (0, width // (half * rank)))
    mirror_weight = jnp.concatenate(mirror_parts, axis=0)
    mirror_back = back_rows(half, cap, got_x[half], mirror_weight, mirror_low, True)
    back[half] = mirror_back[0]
    for at, s in enumerate(range(half + 1 + half // 2, count_blk)):
        got_x[s] = far.swap(sent_x[s], s)
        for partner in (2 * at + 1, 2 * at + 2):
            back[half + partner] = near.swap(mirror_back[partner], partner)
    for partner in range(1, half):
        if half + partner not in back:
            back[half + partner] = near.swap(mirror_back[partner], partner)

    blocks_x = [got_x[s] for s in range(count_blk)]
    hidden, gram_x, live = rows_products(blocks_x, down_weight, 1.0, with_extra=True)
    amount = jnp.sum(live[:, 0], dtype=jnp.float32).reshape(1, 1)
    left_a, left_b, local_sq = fold(amount, grad_hidden, gram_x, hidden, gram_dy)
    factor = clip_factor(local_sq, adapters, rank, width)
    grad_a, grad_b = grads(factor, left_a, left_b, blocks_x, blocks_dy, width)
    input_grad = input_grad_of(cap, me, owner, tenant, [back[s] for s in range(count_blk)])
    return (input_grad, grad_a[None], grad_b[None])


def per_device(tokens, cotangent, tenant, owner, down_factor_table, up_factor_table):
    rows, width = tokens.shape
    count_blk = lax.axis_size("blk")
    adapters = owner.shape[0]
    rank = down_factor_table.shape[1]
    cap = 2 * rows // adapters
    slots = count_blk * cap
    down_weight = down_factor_table[0]
    up_weight = up_factor_table[0]

    with jax.named_scope("targets"):
        tenant_ids = tenant[:, 0]
        match = tenant_ids[:, None] == jnp.arange(adapters, dtype=jnp.int32)[None, :]
        target_dev = jnp.sum(jnp.where(match, owner[None, :], 0), axis=1)
        row_ids = jnp.arange(rows, dtype=jnp.int32)
        same_before = (tenant_ids[:, None] == tenant_ids[None, :]) & (row_ids[None, :] < row_ids[:, None])
        position = jnp.sum(same_before.astype(jnp.int32), axis=1)
        target = target_dev * cap + position
        placing = (jnp.arange(slots, dtype=jnp.int32)[:, None] == target[None, :]).astype(jnp.bfloat16)

    def exchange(value):
        value = value.reshape(count_blk, cap, width)
        return lax.all_to_all(value, "blk", split_axis=0, concat_axis=0, tiled=True).reshape(slots, width)

    def place(value):
        return jnp.dot(placing, value, preferred_element_type=jnp.float32).astype(jnp.bfloat16)

    with jax.named_scope("send_cotangent"):
        rows_dy = exchange(place(cotangent))
    with jax.named_scope("send_tokens"):
        rows_x = exchange(place(tokens))
    with jax.named_scope("row_counts"):
        devices = jnp.arange(count_blk, dtype=jnp.int32)
        sent = jnp.sum((target_dev[:, None] == devices[None, :]).astype(jnp.float32), axis=0, keepdims=True)
        counts = total_over_blk(sent)
        amount = jnp.sum(jnp.where(devices == lax.axis_index("blk"), counts[0], 0.0)).reshape(1, 1)
    with jax.named_scope("grad_hidden"):
        grad_hidden, gram_dy = rows_products([rows_dy], up_weight, SCALE)
    with jax.named_scope("back"):
        back = jnp.dot(grad_hidden, down_weight, preferred_element_type=jnp.float32).astype(jnp.bfloat16)
        returned = exchange(back)
    with jax.named_scope("hidden"):
        hidden, gram_x = rows_products([rows_x], down_weight, 1.0)
    with jax.named_scope("fold"):
        left_a, left_b, local_sq = fold(amount, grad_hidden, gram_x, hidden, gram_dy)
    with jax.named_scope("clip"):
        factor = clip_factor(local_sq, adapters, rank, width)
    with jax.named_scope("grads"):
        grad_a, grad_b = grads(factor, left_a, left_b, [rows_x], [rows_dy], width)
    with jax.named_scope("input_grad"):
        input_grad = lax.dot_general(placing, returned, FIRST, preferred_element_type=jnp.float32).astype(
            jnp.bfloat16
        )
    return (input_grad, grad_a[None], grad_b[None])


def solution(mesh):
    body = per_device_blocks if mesh.shape["blk"] == 16 else per_device
    split = ("groups", "blk")
    in_specs = (P(split, None), P(split, None), P(split, None), P("groups"), P(split, None, None), P(split, None, None))
    out_specs = (P(split, None), P(split, None, None), P(split, None, None))
    return jax.shard_map(body, mesh=mesh, in_specs=in_specs, out_specs=out_specs, check_vma=False)
```

```python
import jax
import jax.numpy as jnp
from jax import lax
from jax.experimental import pallas as pl
from jax.experimental.pallas import tpu as pltpu
from jax.sharding import PartitionSpec as P

SCALE = 2.0
DAMPING = 1.0
EPS = 1e-06
VMEM_LIMIT = 44 * 1024 * 1024
LANES = 128
FAR_WINDOW = 4
CHUNK = 8192
MIRROR_ORDER = [1, 2, 3, 4, 5, 6, 7]
NEAR_WINDOW = 4
LAST = (((1,), (1,)), ((), ()))
FIRST = (((0,), (0,)), ((), ()))


def total_over_blk(value):
    size = lax.axis_size("blk")
    if size & (size - 1):
        return lax.psum(value, "blk")
    step = 1
    while step < size:
        value = value + lax.ppermute(value, "blk", [(i, i ^ step) for i in range(size)])
        step *= 2
    return value


def rows_kernel(scale, count, with_extra, *refs):
    blocks, (weight_ref, low_ref, gram_ref, *rest) = refs[:count], refs[count:]
    low_total = rest[-1]
    step = pl.program_id(0)
    chunk = weight_ref.shape[1]

    @pl.when(step == 0)
    def _():
        low_total[...] = jnp.zeros_like(low_total)
        gram_ref[...] = jnp.zeros_like(gram_ref)
        if with_extra:
            rest[0][...] = jnp.concatenate([ref[:, ref.shape[1] - LANES :] for ref in blocks], axis=0)

    rows = jnp.concatenate([ref[:, :chunk] for ref in blocks], axis=0)
    low_total[...] += lax.dot_general(rows, weight_ref[...], LAST, preferred_element_type=jnp.float32)
    gram_ref[...] += lax.dot_general(rows, rows, LAST, preferred_element_type=jnp.float32)

    @pl.when(step == pl.num_programs(0) - 1)
    def _():
        low_ref[...] = (scale * low_total[...]).astype(low_ref.dtype)


def rows_products(blocks, weight, scale, with_extra=False):
    slots = sum(block.shape[0] for block in blocks)
    rank, width = weight.shape
    chunk = width if with_extra else min(width, CHUNK)
    in_specs = [
        pl.BlockSpec((block.shape[0], block.shape[1] if with_extra else chunk), lambda i: (0, i)) for block in blocks
    ]
    out_specs = [pl.BlockSpec((slots, rank), lambda i: (0, 0)), pl.BlockSpec((slots, slots), lambda i: (0, 0))]
    out_shape = [
        jax.ShapeDtypeStruct((slots, rank), jnp.bfloat16),
        jax.ShapeDtypeStruct((slots, slots), jnp.float32),
    ]
    if with_extra:
        out_specs.append(pl.BlockSpec((slots, LANES), lambda i: (0, 0)))
        out_shape.append(jax.ShapeDtypeStruct((slots, LANES), jnp.bfloat16))
    return pl.pallas_call(
        lambda *refs: rows_kernel(scale, len(blocks), with_extra, *refs),
        grid=(width // chunk,),
        in_specs=in_specs + [pl.BlockSpec((rank, chunk), lambda i: (0, i))],
        out_specs=out_specs,
        out_shape=out_shape,
        scratch_shapes=[pltpu.VMEM((slots, rank), jnp.float32)],
        compiler_params=pltpu.CompilerParams(vmem_limit_bytes=VMEM_LIMIT),
        cost_estimate=pl.CostEstimate(
            flops=2 * slots * width * (slots + rank),
            bytes_accessed=2 * width * (slots + rank),
            transcendentals=0,
        ),
    )(*blocks, weight)


def slot_targets(cap, me, owner_ref, column_ref, row_ref):
    column, row = column_ref[...], row_ref[...]
    rows, adapters = row.shape[1], owner_ref.shape[0]
    adapter = lax.broadcasted_iota(jnp.int32, (adapters, rows), 0)
    device = jnp.sum(jnp.where(adapter == row, owner_ref[...], 0), axis=0, keepdims=True)
    earlier = lax.broadcasted_iota(jnp.int32, (rows, rows), 0) < lax.broadcasted_iota(jnp.int32, (rows, rows), 1)
    position = jnp.sum(jnp.where((column == row) & earlier, 1, 0), axis=0, keepdims=True)
    partner = device ^ me
    return partner, partner * cap + position


def place_kernel(partners, cap, with_live, me_ref, owner_ref, column_ref, row_ref, values_ref, *refs):
    placing = refs[-1]
    low_refs, outs = refs[: len(refs) - 1 - len(partners)], refs[len(refs) - 1 - len(partners) : -1]
    step = pl.program_id(0)
    rows, chunk = row_ref.shape[1], values_ref.shape[1]

    @pl.when(step == 0)
    def _():
        _, target = slot_targets(cap, me_ref[0, 0], owner_ref, column_ref, row_ref)
        slot = lax.broadcasted_iota(jnp.int32, (cap, rows), 0)
        for at, partner in enumerate(partners):
            placing[at * cap : (at + 1) * cap, :] = jnp.where(slot + partner * cap == target, 1.0, 0.0).astype(
                placing.dtype
            )

    placed = jnp.dot(placing[...], values_ref[...], preferred_element_type=jnp.float32).astype(jnp.bfloat16)
    for at, out in enumerate(outs):
        if with_live:
            out[:, pl.ds(pl.multiple_of(step * chunk, chunk), chunk)] = placed[at * cap : (at + 1) * cap]
        else:
            out[...] = placed[at * cap : (at + 1) * cap]

    if with_live:

        @pl.when(step == pl.num_programs(0) - 1)
        def _():
            live = jnp.sum(placing[...].astype(jnp.float32), axis=1, keepdims=True).astype(jnp.bfloat16)
            for at, out in enumerate(outs):
                full = out.shape[1]
                out[:, full - LANES :] = jnp.broadcast_to(live[at * cap : (at + 1) * cap], (cap, LANES))
                if low_refs:
                    low = low_refs[0][...].astype(jnp.float32)
                    lanes = [low[q * cap : (q + 1) * cap] for q in range(low.shape[0] // cap)]
                    out[:, pl.num_programs(0) * chunk : full - LANES] = jnp.concatenate(lanes, axis=1).astype(
                        jnp.bfloat16
                    )


def place(partners, cap, me, owner, tenant, values, with_live=False, low=None):
    rows, width = values.shape
    adapters = owner.shape[0]
    full = width + (LANES if with_live else 0) + (low.size // cap if low is not None else 0)
    chunk = min(width, CHUNK)
    still = lambda shape: pl.BlockSpec(shape, lambda i: (0, 0))
    in_specs = [
        pl.BlockSpec(memory_space=pltpu.SMEM),
        still((adapters, 1)),
        still((rows, 1)),
        still((1, rows)),
        pl.BlockSpec((rows, chunk), lambda i: (0, i)),
    ]
    operands = [me.reshape(1, 1), owner.reshape(adapters, 1), tenant, tenant.reshape(1, rows), values]
    if low is not None:
        in_specs.append(still(low.shape))
        operands.append(low)
    out_spec = still((cap, full)) if with_live else pl.BlockSpec((cap, chunk), lambda i: (0, i))
    return pl.pallas_call(
        lambda *refs: place_kernel(partners, cap, with_live, *refs),
        grid=(width // chunk,),
        in_specs=in_specs,
        out_specs=[out_spec] * len(partners),
        out_shape=[jax.ShapeDtypeStruct((cap, full), jnp.bfloat16)] * len(partners),
        scratch_shapes=[pltpu.VMEM((len(partners) * cap, rows), jnp.bfloat16)],
        compiler_params=pltpu.CompilerParams(vmem_limit_bytes=VMEM_LIMIT),
        cost_estimate=pl.CostEstimate(
            flops=2 * len(partners) * cap * rows * width,
            bytes_accessed=2 * width * (rows + len(partners) * cap),
            transcendentals=0,
        ),
    )(*operands)


def back_kernel(count, stacked, low_ref, weight_ref, *outs):
    cap = outs[0].shape[0]
    rank = weight_ref.shape[0]
    if stacked:
        low = low_ref[...].astype(jnp.float32)
        low = jnp.concatenate([low[:, at * rank : (at + 1) * rank] for at in range(count)], axis=0)
        low = low.astype(jnp.bfloat16)
    else:
        low = low_ref[...]
    rows = jnp.dot(low, weight_ref[...], preferred_element_type=jnp.float32).astype(jnp.bfloat16)
    for at, out in enumerate(outs):
        out[...] = rows[at * cap : (at + 1) * cap]


def back_rows(count, cap, low, weight, low_spec, stacked):
    rank, width = weight.shape
    chunk = min(width, CHUNK)
    return pl.pallas_call(
        lambda *refs: back_kernel(count, stacked, *refs),
        grid=(width // chunk,),
        in_specs=[low_spec, pl.BlockSpec((rank, chunk), lambda i: (0, i))],
        out_specs=[pl.BlockSpec((cap, chunk), lambda i: (0, i))] * count,
        out_shape=[jax.ShapeDtypeStruct((cap, width), jnp.bfloat16)] * count,
        compiler_params=pltpu.CompilerParams(vmem_limit_bytes=VMEM_LIMIT),
        cost_estimate=pl.CostEstimate(
            flops=2 * count * cap * rank * width, bytes_accessed=2 * width * (rank + count * cap), transcendentals=0
        ),
    )(low, weight)


def input_grad_kernel(cap, count, me_ref, owner_ref, column_ref, row_ref, *refs):
    blocks, out_ref, placing = refs[:count], refs[count], refs[count + 1]
    step = pl.program_id(0)

    @pl.when(step == 0)
    def _():
        _, target = slot_targets(cap, me_ref[0, 0], owner_ref, column_ref, row_ref)
        slot = lax.broadcasted_iota(jnp.int32, placing.shape, 0)
        placing[...] = jnp.where(slot == target, 1.0, 0.0).astype(placing.dtype)

    returned = jnp.concatenate([ref[...] for ref in blocks], axis=0)
    out_ref[...] = lax.dot_general(placing[...], returned, FIRST, preferred_element_type=jnp.float32).astype(
        out_ref.dtype
    )


def input_grad_of(cap, me, owner, tenant, blocks):
    rows, adapters, count = tenant.shape[0], owner.shape[0], len(blocks)
    width = blocks[0].shape[1]
    chunk = min(width, CHUNK)
    still = lambda shape: pl.BlockSpec(shape, lambda i: (0, 0))
    return pl.pallas_call(
        lambda *refs: input_grad_kernel(cap, count, *refs),
        grid=(width // chunk,),
        in_specs=[
            pl.BlockSpec(memory_space=pltpu.SMEM),
            still((adapters, 1)),
            still((rows, 1)),
            still((1, rows)),
        ]
        + [pl.BlockSpec((cap, chunk), lambda i: (0, i))] * count,
        out_specs=pl.BlockSpec((rows, chunk), lambda i: (0, i)),
        out_shape=jax.ShapeDtypeStruct((rows, width), jnp.bfloat16),
        scratch_shapes=[pltpu.VMEM((count * cap, rows), jnp.bfloat16)],
        compiler_params=pltpu.CompilerParams(vmem_limit_bytes=VMEM_LIMIT),
        cost_estimate=pl.CostEstimate(
            flops=2 * rows * count * cap * width,
            bytes_accessed=2 * width * (rows + count * cap),
            transcendentals=0,
        ),
    )(me.reshape(1, 1), owner.reshape(adapters, 1), tenant, tenant.reshape(1, rows), *blocks)


def fold_one(low, gram, scale, amount):
    high = lax.Precision.HIGHEST
    low = low.astype(jnp.float32)
    slots = low.shape[0]
    left = jnp.sum(low, axis=0, keepdims=True) / amount
    raw = scale * low
    along = jnp.sum(raw * left, axis=1, keepdims=True)
    inner = raw - along * left / (DAMPING + jnp.sum(left * left))
    cross = jnp.sum(gram, axis=1, keepdims=True) / amount
    right_sq = jnp.sum(cross) / amount
    side = jnp.sum(inner * cross, axis=0, keepdims=True)
    factor = inner - side / (amount * (DAMPING + right_sq))
    spread = jnp.dot(gram, factor, precision=high, preferred_element_type=jnp.float32)
    return factor, jnp.sum(spread * factor)


def split3(value):
    first = value.astype(jnp.bfloat16)
    rest = value - first.astype(jnp.float32)
    second = rest.astype(jnp.bfloat16)
    third = (rest - second.astype(jnp.float32)).astype(jnp.bfloat16)
    return first, second, third


def fold_kernel(amount_ref, gh_ref, gram_x_ref, hidden_ref, gram_dy_ref, left_a_ref, left_b_ref, sq_ref):
    amount = amount_ref[0, 0]
    rank = gh_ref.shape[1]
    factor_a, sq_a = fold_one(gh_ref[...], gram_x_ref[...], 1.0, amount)
    factor_b, sq_b = fold_one(hidden_ref[...], gram_dy_ref[...], SCALE, amount)
    for out_ref, factor in ((left_a_ref, factor_a), (left_b_ref, factor_b)):
        for at, part in enumerate(split3(factor)):
            out_ref[:, at * rank : (at + 1) * rank] = part
    sq_ref[...] = jnp.zeros_like(sq_ref) + (sq_a + sq_b)


def fold(amount, grad_hidden, gram_x, hidden, gram_dy):
    slots, rank = hidden.shape
    whole = lambda shape: pl.BlockSpec(shape, lambda: (0, 0))
    return pl.pallas_call(
        fold_kernel,
        in_specs=[pl.BlockSpec(memory_space=pltpu.SMEM)]
        + [whole((slots, rank)), whole((slots, slots))] * 2,
        out_specs=[whole((slots, 3 * rank))] * 2 + [whole((8, 128))],
        out_shape=[jax.ShapeDtypeStruct((slots, 3 * rank), jnp.bfloat16)] * 2
        + [jax.ShapeDtypeStruct((8, 128), jnp.float32)],
        compiler_params=pltpu.CompilerParams(vmem_limit_bytes=VMEM_LIMIT),
        cost_estimate=pl.CostEstimate(
            flops=24 * slots * slots * rank, bytes_accessed=12 * slots * slots, transcendentals=0
        ),
    )(amount, grad_hidden, gram_x, hidden, gram_dy)


def grads_kernel(count, factor_ref, left_a_ref, left_b_ref, *refs):
    blocks_x, blocks_dy = refs[:count], refs[count : 2 * count]
    grad_a_ref, grad_b_ref = refs[2 * count :]
    factor = factor_ref[0, 0]
    rank = grad_a_ref.shape[0]
    for left_ref, blocks, out_ref in ((left_a_ref, blocks_x, grad_a_ref), (left_b_ref, blocks_dy, grad_b_ref)):
        rows = jnp.concatenate([ref[...] for ref in blocks], axis=0)
        parts = lax.dot_general(left_ref[...], rows, FIRST, preferred_element_type=jnp.float32)
        proj = (parts[2 * rank :] + parts[rank : 2 * rank]) + parts[:rank]
        out_ref[...] = (factor * proj).astype(out_ref.dtype)


def grads(factor, left_a, left_b, blocks_x, blocks_dy, width):
    slots = left_a.shape[0]
    rank = left_a.shape[1] // 3
    chunk = min(width, CHUNK)
    left_spec = pl.BlockSpec((slots, 3 * rank), lambda i: (0, 0))
    rows_specs = [pl.BlockSpec((block.shape[0], chunk), lambda i: (0, i)) for block in blocks_x]
    out_spec = pl.BlockSpec((rank, chunk), lambda i: (0, i))
    return pl.pallas_call(
        lambda *refs: grads_kernel(len(blocks_x), *refs),
        grid=(width // chunk,),
        in_specs=[pl.BlockSpec(memory_space=pltpu.SMEM), left_spec, left_spec] + rows_specs * 2,
        out_specs=[out_spec, out_spec],
        out_shape=[jax.ShapeDtypeStruct((rank, width), jnp.bfloat16)] * 2,
        compiler_params=pltpu.CompilerParams(vmem_limit_bytes=VMEM_LIMIT),
        cost_estimate=pl.CostEstimate(
            flops=12 * slots * width * rank, bytes_accessed=4 * width * (slots + rank), transcendentals=0
        ),
    )(factor, left_a, left_b, *blocks_x, *blocks_dy)


def clip_factor(local_sq, adapters, rank, width):
    total = total_over_blk(local_sq[:1, :1])
    mean_sq = total / (2.0 * adapters * rank * width)
    return jnp.minimum(1.0, 1.0 / jnp.sqrt(mean_sq + EPS))


class Line:
    def __init__(self, window):
        self.window = window
        self.results = []

    def swap(self, value, partner):
        if len(self.results) >= self.window:
            value, _ = lax.optimization_barrier((value, self.results[-self.window]))
        size = lax.axis_size("blk")
        result = lax.ppermute(value, "blk", [(i, i ^ partner) for i in range(size)])
        self.results.append(result)
        return result


def per_device_blocks(tokens, cotangent, tenant, owner, down_factor_table, up_factor_table):
    rows, width = tokens.shape
    count_blk = lax.axis_size("blk")
    half = count_blk // 2
    adapters = owner.shape[0]
    rank = down_factor_table.shape[1]
    cap = 2 * rows // adapters
    down_weight = down_factor_table[0]
    up_weight = up_factor_table[0]
    me = lax.axis_index("blk").astype(jnp.int32)
    far, near = Line(FAR_WINDOW), Line(NEAR_WINDOW)
    low_of = lambda low, first, count: low[first * cap : (first + count) * cap]
    parts = rank // cap
    mirror_parts = []

    def send_weight(number):
        for _ in range(number):
            at = len(mirror_parts)
            mirror_parts.append(far.swap(down_weight[at * cap : (at + 1) * cap], half))

    send_weight(parts // 2)
    sent_dy = place(list(range(count_blk)), cap, me, owner, tenant, cotangent)
    others = [s for s in range(count_blk) if s != half]
    sent_x = dict(zip(others, place(others, cap, me, owner, tenant, tokens, with_live=True)))
    got_dy, got_x = {0: sent_dy[0]}, {0: sent_x[0]}
    near_queue = [(got_dy, sent_dy, s) for s in range(1, half)] + [(got_x, sent_x, s) for s in range(1, half)]
    for s in range(half, count_blk):
        got_dy[s] = far.swap(sent_dy[s], s)
        for got, sent, partner in near_queue[:2]:
            got[partner] = near.swap(sent[partner], partner)
        del near_queue[:2]
    send_weight(parts - len(mirror_parts))

    blocks_dy = [got_dy[s] for s in range(count_blk)]
    grad_hidden, gram_dy = rows_products(blocks_dy, up_weight, SCALE)
    (sent_mirror,) = place(
        [half], cap, me, owner, tenant, tokens, with_live=True, low=low_of(grad_hidden, half, half)
    )
    still = pl.BlockSpec((half * cap, rank), lambda i: (0, 0))
    own_back = back_rows(half, cap, low_of(grad_hidden, 0, half), down_weight, still, False)
    back = {0: own_back[0]}
    got_x[half + 1] = far.swap(sent_x[half + 1], half + 1)
    got_x[half] = far.swap(sent_mirror, half)
    for s in range(1, half // 2):
        got_x[half + 1 + s] = far.swap(sent_x[half + 1 + s], half + 1 + s)
        for at in (2 * s - 1, 2 * s):
            back[at] = near.swap(own_back[at], at)
    back[half - 1] = near.swap(own_back[half - 1], half - 1)
    mirror_low = pl.BlockSpec((cap, half * rank), lambda i: (0, width // (half * rank)))
    mirror_weight = jnp.concatenate(mirror_parts, axis=0)
    mirror_back = back_rows(half, cap, got_x[half], mirror_weight, mirror_low, True)
    back[half] = mirror_back[0]
    for at, s in enumerate(range(half + 1 + half // 2, count_blk)):
        got_x[s] = far.swap(sent_x[s], s)
        for partner in MIRROR_ORDER[2 * at : 2 * at + 2]:
            back[half + partner] = near.swap(mirror_back[partner], partner)
    for partner in MIRROR_ORDER[6:]:
        back[half + partner] = near.swap(mirror_back[partner], partner)

    blocks_x = [got_x[s] for s in range(count_blk)]
    hidden, gram_x, live = rows_products(blocks_x, down_weight, 1.0, with_extra=True)
    amount = jnp.sum(live[:, 0], dtype=jnp.float32).reshape(1, 1)
    left_a, left_b, local_sq = fold(amount, grad_hidden, gram_x, hidden, gram_dy)
    factor = clip_factor(local_sq, adapters, rank, width)
    grad_a, grad_b = grads(factor, left_a, left_b, blocks_x, blocks_dy, width)
    input_grad = input_grad_of(cap, me, owner, tenant, [back[s] for s in range(count_blk)])
    return (input_grad, grad_a[None], grad_b[None])


def per_device(tokens, cotangent, tenant, owner, down_factor_table, up_factor_table):
    rows, width = tokens.shape
    count_blk = lax.axis_size("blk")
    adapters = owner.shape[0]
    rank = down_factor_table.shape[1]
    cap = 2 * rows // adapters
    slots = count_blk * cap
    down_weight = down_factor_table[0]
    up_weight = up_factor_table[0]

    with jax.named_scope("targets"):
        tenant_ids = tenant[:, 0]
        match = tenant_ids[:, None] == jnp.arange(adapters, dtype=jnp.int32)[None, :]
        target_dev = jnp.sum(jnp.where(match, owner[None, :], 0), axis=1)
        row_ids = jnp.arange(rows, dtype=jnp.int32)
        same_before = (tenant_ids[:, None] == tenant_ids[None, :]) & (row_ids[None, :] < row_ids[:, None])
        position = jnp.sum(same_before.astype(jnp.int32), axis=1)
        target = target_dev * cap + position
        placing = (jnp.arange(slots, dtype=jnp.int32)[:, None] == target[None, :]).astype(jnp.bfloat16)

    def exchange(value):
        value = value.reshape(count_blk, cap, width)
        return lax.all_to_all(value, "blk", split_axis=0, concat_axis=0, tiled=True).reshape(slots, width)

    def place(value):
        return jnp.dot(placing, value, preferred_element_type=jnp.float32).astype(jnp.bfloat16)

    with jax.named_scope("send_cotangent"):
        rows_dy = exchange(place(cotangent))
    with jax.named_scope("send_tokens"):
        rows_x = exchange(place(tokens))
    with jax.named_scope("row_counts"):
        devices = jnp.arange(count_blk, dtype=jnp.int32)
        sent = jnp.sum((target_dev[:, None] == devices[None, :]).astype(jnp.float32), axis=0, keepdims=True)
        counts = total_over_blk(sent)
        amount = jnp.sum(jnp.where(devices == lax.axis_index("blk"), counts[0], 0.0)).reshape(1, 1)
    with jax.named_scope("grad_hidden"):
        grad_hidden, gram_dy = rows_products([rows_dy], up_weight, SCALE)
    with jax.named_scope("back"):
        back = jnp.dot(grad_hidden, down_weight, preferred_element_type=jnp.float32).astype(jnp.bfloat16)
        returned = exchange(back)
    with jax.named_scope("hidden"):
        hidden, gram_x = rows_products([rows_x], down_weight, 1.0)
    with jax.named_scope("fold"):
        left_a, left_b, local_sq = fold(amount, grad_hidden, gram_x, hidden, gram_dy)
    with jax.named_scope("clip"):
        factor = clip_factor(local_sq, adapters, rank, width)
    with jax.named_scope("grads"):
        grad_a, grad_b = grads(factor, left_a, left_b, [rows_x], [rows_dy], width)
    with jax.named_scope("input_grad"):
        input_grad = lax.dot_general(placing, returned, FIRST, preferred_element_type=jnp.float32).astype(
            jnp.bfloat16
        )
    return (input_grad, grad_a[None], grad_b[None])


def solution(mesh):
    body = per_device_blocks if mesh.shape["blk"] == 16 else per_device
    split = ("groups", "blk")
    in_specs = (P(split, None), P(split, None), P(split, None), P("groups"), P(split, None, None), P(split, None, None))
    out_specs = (P(split, None), P(split, None, None), P(split, None, None))
    return jax.shard_map(body, mesh=mesh, in_specs=in_specs, out_specs=out_specs, check_vma=False)
```

```python
import jax
import jax.numpy as jnp
from jax import lax
from jax.experimental import pallas as pl
from jax.experimental.pallas import tpu as pltpu
from jax.sharding import PartitionSpec as P

SCALE = 2.0
DAMPING = 1.0
EPS = 1e-06
VMEM_LIMIT = 44 * 1024 * 1024
LANES = 128
FAR_WINDOW = 4
CHUNK = 8192
WEIGHT_FIRST = 2
RATE = 1
WEIGHT_MID = 11
MIRROR_ORDER = [1, 2, 3, 4, 5, 6, 7]
NEAR_WINDOW = 4
LAST = (((1,), (1,)), ((), ()))
FIRST = (((0,), (0,)), ((), ()))


def total_over_blk(value):
    size = lax.axis_size("blk")
    if size & (size - 1):
        return lax.psum(value, "blk")
    step = 1
    while step < size:
        value = value + lax.ppermute(value, "blk", [(i, i ^ step) for i in range(size)])
        step *= 2
    return value


def rows_kernel(scale, count, with_extra, *refs):
    blocks, (weight_ref, low_ref, gram_ref, *rest) = refs[:count], refs[count:]
    low_total = rest[-1]
    step = pl.program_id(0)
    chunk = weight_ref.shape[1]

    @pl.when(step == 0)
    def _():
        low_total[...] = jnp.zeros_like(low_total)
        gram_ref[...] = jnp.zeros_like(gram_ref)
        if with_extra:
            rest[0][...] = jnp.concatenate([ref[:, ref.shape[1] - LANES :] for ref in blocks], axis=0)

    rows = jnp.concatenate([ref[:, :chunk] for ref in blocks], axis=0)
    low_total[...] += lax.dot_general(rows, weight_ref[...], LAST, preferred_element_type=jnp.float32)
    gram_ref[...] += lax.dot_general(rows, rows, LAST, preferred_element_type=jnp.float32)

    @pl.when(step == pl.num_programs(0) - 1)
    def _():
        low_ref[...] = (scale * low_total[...]).astype(low_ref.dtype)


def rows_products(blocks, weight, scale, with_extra=False):
    slots = sum(block.shape[0] for block in blocks)
    rank, width = weight.shape
    chunk = width if with_extra else min(width, CHUNK)
    in_specs = [
        pl.BlockSpec((block.shape[0], block.shape[1] if with_extra else chunk), lambda i: (0, i)) for block in blocks
    ]
    out_specs = [pl.BlockSpec((slots, rank), lambda i: (0, 0)), pl.BlockSpec((slots, slots), lambda i: (0, 0))]
    out_shape = [
        jax.ShapeDtypeStruct((slots, rank), jnp.bfloat16),
        jax.ShapeDtypeStruct((slots, slots), jnp.float32),
    ]
    if with_extra:
        out_specs.append(pl.BlockSpec((slots, LANES), lambda i: (0, 0)))
        out_shape.append(jax.ShapeDtypeStruct((slots, LANES), jnp.bfloat16))
    return pl.pallas_call(
        lambda *refs: rows_kernel(scale, len(blocks), with_extra, *refs),
        grid=(width // chunk,),
        in_specs=in_specs + [pl.BlockSpec((rank, chunk), lambda i: (0, i))],
        out_specs=out_specs,
        out_shape=out_shape,
        scratch_shapes=[pltpu.VMEM((slots, rank), jnp.float32)],
        compiler_params=pltpu.CompilerParams(vmem_limit_bytes=VMEM_LIMIT),
        cost_estimate=pl.CostEstimate(
            flops=2 * slots * width * (slots + rank),
            bytes_accessed=2 * width * (slots + rank),
            transcendentals=0,
        ),
    )(*blocks, weight)


def slot_targets(cap, me, owner_ref, column_ref, row_ref):
    column, row = column_ref[...], row_ref[...]
    rows, adapters = row.shape[1], owner_ref.shape[0]
    adapter = lax.broadcasted_iota(jnp.int32, (adapters, rows), 0)
    device = jnp.sum(jnp.where(adapter == row, owner_ref[...], 0), axis=0, keepdims=True)
    earlier = lax.broadcasted_iota(jnp.int32, (rows, rows), 0) < lax.broadcasted_iota(jnp.int32, (rows, rows), 1)
    position = jnp.sum(jnp.where((column == row) & earlier, 1, 0), axis=0, keepdims=True)
    partner = device ^ me
    return partner, partner * cap + position


def place_kernel(partners, cap, with_live, me_ref, owner_ref, column_ref, row_ref, values_ref, *refs):
    placing = refs[-1]
    low_refs, outs = refs[: len(refs) - 1 - len(partners)], refs[len(refs) - 1 - len(partners) : -1]
    step = pl.program_id(0)
    rows, chunk = row_ref.shape[1], values_ref.shape[1]

    @pl.when(step == 0)
    def _():
        _, target = slot_targets(cap, me_ref[0, 0], owner_ref, column_ref, row_ref)
        slot = lax.broadcasted_iota(jnp.int32, (cap, rows), 0)
        for at, partner in enumerate(partners):
            placing[at * cap : (at + 1) * cap, :] = jnp.where(slot + partner * cap == target, 1.0, 0.0).astype(
                placing.dtype
            )

    placed = jnp.dot(placing[...], values_ref[...], preferred_element_type=jnp.float32).astype(jnp.bfloat16)
    for at, out in enumerate(outs):
        if with_live:
            out[:, pl.ds(pl.multiple_of(step * chunk, chunk), chunk)] = placed[at * cap : (at + 1) * cap]
        else:
            out[...] = placed[at * cap : (at + 1) * cap]

    if with_live:

        @pl.when(step == pl.num_programs(0) - 1)
        def _():
            live = jnp.sum(placing[...].astype(jnp.float32), axis=1, keepdims=True).astype(jnp.bfloat16)
            for at, out in enumerate(outs):
                full = out.shape[1]
                out[:, full - LANES :] = jnp.broadcast_to(live[at * cap : (at + 1) * cap], (cap, LANES))
                if low_refs:
                    low = low_refs[0][...].astype(jnp.float32)
                    lanes = [low[q * cap : (q + 1) * cap] for q in range(low.shape[0] // cap)]
                    out[:, pl.num_programs(0) * chunk : full - LANES] = jnp.concatenate(lanes, axis=1).astype(
                        jnp.bfloat16
                    )


def place(partners, cap, me, owner, tenant, values, with_live=False, low=None):
    rows, width = values.shape
    adapters = owner.shape[0]
    full = width + (LANES if with_live else 0) + (low.size // cap if low is not None else 0)
    chunk = min(width, CHUNK)
    still = lambda shape: pl.BlockSpec(shape, lambda i: (0, 0))
    in_specs = [
        pl.BlockSpec(memory_space=pltpu.SMEM),
        still((adapters, 1)),
        still((rows, 1)),
        still((1, rows)),
        pl.BlockSpec((rows, chunk), lambda i: (0, i)),
    ]
    operands = [me.reshape(1, 1), owner.reshape(adapters, 1), tenant, tenant.reshape(1, rows), values]
    if low is not None:
        in_specs.append(still(low.shape))
        operands.append(low)
    out_spec = still((cap, full)) if with_live else pl.BlockSpec((cap, chunk), lambda i: (0, i))
    return pl.pallas_call(
        lambda *refs: place_kernel(partners, cap, with_live, *refs),
        grid=(width // chunk,),
        in_specs=in_specs,
        out_specs=[out_spec] * len(partners),
        out_shape=[jax.ShapeDtypeStruct((cap, full), jnp.bfloat16)] * len(partners),
        scratch_shapes=[pltpu.VMEM((len(partners) * cap, rows), jnp.bfloat16)],
        compiler_params=pltpu.CompilerParams(vmem_limit_bytes=VMEM_LIMIT),
        cost_estimate=pl.CostEstimate(
            flops=2 * len(partners) * cap * rows * width,
            bytes_accessed=2 * width * (rows + len(partners) * cap),
            transcendentals=0,
        ),
    )(*operands)


def back_kernel(count, stacked, low_ref, weight_ref, *outs):
    cap = outs[0].shape[0]
    rank = weight_ref.shape[0]
    if stacked:
        low = low_ref[...].astype(jnp.float32)
        low = jnp.concatenate([low[:, at * rank : (at + 1) * rank] for at in range(count)], axis=0)
        low = low.astype(jnp.bfloat16)
    else:
        low = low_ref[...]
    rows = jnp.dot(low, weight_ref[...], preferred_element_type=jnp.float32).astype(jnp.bfloat16)
    for at, out in enumerate(outs):
        out[...] = rows[at * cap : (at + 1) * cap]


def back_rows(count, cap, low, weight, low_spec, stacked):
    rank, width = weight.shape
    chunk = min(width, CHUNK)
    return pl.pallas_call(
        lambda *refs: back_kernel(count, stacked, *refs),
        grid=(width // chunk,),
        in_specs=[low_spec, pl.BlockSpec((rank, chunk), lambda i: (0, i))],
        out_specs=[pl.BlockSpec((cap, chunk), lambda i: (0, i))] * count,
        out_shape=[jax.ShapeDtypeStruct((cap, width), jnp.bfloat16)] * count,
        compiler_params=pltpu.CompilerParams(vmem_limit_bytes=VMEM_LIMIT),
        cost_estimate=pl.CostEstimate(
            flops=2 * count * cap * rank * width, bytes_accessed=2 * width * (rank + count * cap), transcendentals=0
        ),
    )(low, weight)


def input_grad_kernel(cap, count, me_ref, owner_ref, column_ref, row_ref, *refs):
    blocks, out_ref, placing = refs[:count], refs[count], refs[count + 1]
    step = pl.program_id(0)

    @pl.when(step == 0)
    def _():
        _, target = slot_targets(cap, me_ref[0, 0], owner_ref, column_ref, row_ref)
        slot = lax.broadcasted_iota(jnp.int32, placing.shape, 0)
        placing[...] = jnp.where(slot == target, 1.0, 0.0).astype(placing.dtype)

    returned = jnp.concatenate([ref[...] for ref in blocks], axis=0)
    out_ref[...] = lax.dot_general(placing[...], returned, FIRST, preferred_element_type=jnp.float32).astype(
        out_ref.dtype
    )


def input_grad_of(cap, me, owner, tenant, blocks):
    rows, adapters, count = tenant.shape[0], owner.shape[0], len(blocks)
    width = blocks[0].shape[1]
    chunk = min(width, CHUNK)
    still = lambda shape: pl.BlockSpec(shape, lambda i: (0, 0))
    return pl.pallas_call(
        lambda *refs: input_grad_kernel(cap, count, *refs),
        grid=(width // chunk,),
        in_specs=[
            pl.BlockSpec(memory_space=pltpu.SMEM),
            still((adapters, 1)),
            still((rows, 1)),
            still((1, rows)),
        ]
        + [pl.BlockSpec((cap, chunk), lambda i: (0, i))] * count,
        out_specs=pl.BlockSpec((rows, chunk), lambda i: (0, i)),
        out_shape=jax.ShapeDtypeStruct((rows, width), jnp.bfloat16),
        scratch_shapes=[pltpu.VMEM((count * cap, rows), jnp.bfloat16)],
        compiler_params=pltpu.CompilerParams(vmem_limit_bytes=VMEM_LIMIT),
        cost_estimate=pl.CostEstimate(
            flops=2 * rows * count * cap * width,
            bytes_accessed=2 * width * (rows + count * cap),
            transcendentals=0,
        ),
    )(me.reshape(1, 1), owner.reshape(adapters, 1), tenant, tenant.reshape(1, rows), *blocks)


def fold_one(low, gram, scale, amount):
    high = lax.Precision.HIGHEST
    low = low.astype(jnp.float32)
    slots = low.shape[0]
    left = jnp.sum(low, axis=0, keepdims=True) / amount
    raw = scale * low
    along = jnp.sum(raw * left, axis=1, keepdims=True)
    inner = raw - along * left / (DAMPING + jnp.sum(left * left))
    cross = jnp.sum(gram, axis=1, keepdims=True) / amount
    right_sq = jnp.sum(cross) / amount
    side = jnp.sum(inner * cross, axis=0, keepdims=True)
    factor = inner - side / (amount * (DAMPING + right_sq))
    spread = jnp.dot(gram, factor, precision=high, preferred_element_type=jnp.float32)
    return factor, jnp.sum(spread * factor)


def split3(value):
    first = value.astype(jnp.bfloat16)
    rest = value - first.astype(jnp.float32)
    second = rest.astype(jnp.bfloat16)
    third = (rest - second.astype(jnp.float32)).astype(jnp.bfloat16)
    return first, second, third


def fold_kernel(amount_ref, gh_ref, gram_x_ref, hidden_ref, gram_dy_ref, left_a_ref, left_b_ref, sq_ref):
    amount = amount_ref[0, 0]
    rank = gh_ref.shape[1]
    factor_a, sq_a = fold_one(gh_ref[...], gram_x_ref[...], 1.0, amount)
    factor_b, sq_b = fold_one(hidden_ref[...], gram_dy_ref[...], SCALE, amount)
    for out_ref, factor in ((left_a_ref, factor_a), (left_b_ref, factor_b)):
        for at, part in enumerate(split3(factor)):
            out_ref[:, at * rank : (at + 1) * rank] = part
    sq_ref[...] = jnp.zeros_like(sq_ref) + (sq_a + sq_b)


def fold(amount, grad_hidden, gram_x, hidden, gram_dy):
    slots, rank = hidden.shape
    whole = lambda shape: pl.BlockSpec(shape, lambda: (0, 0))
    return pl.pallas_call(
        fold_kernel,
        in_specs=[pl.BlockSpec(memory_space=pltpu.SMEM)]
        + [whole((slots, rank)), whole((slots, slots))] * 2,
        out_specs=[whole((slots, 3 * rank))] * 2 + [whole((8, 128))],
        out_shape=[jax.ShapeDtypeStruct((slots, 3 * rank), jnp.bfloat16)] * 2
        + [jax.ShapeDtypeStruct((8, 128), jnp.float32)],
        compiler_params=pltpu.CompilerParams(vmem_limit_bytes=VMEM_LIMIT),
        cost_estimate=pl.CostEstimate(
            flops=24 * slots * slots * rank, bytes_accessed=12 * slots * slots, transcendentals=0
        ),
    )(amount, grad_hidden, gram_x, hidden, gram_dy)


def grads_kernel(count, factor_ref, left_a_ref, left_b_ref, *refs):
    blocks_x, blocks_dy = refs[:count], refs[count : 2 * count]
    grad_a_ref, grad_b_ref = refs[2 * count :]
    factor = factor_ref[0, 0]
    rank = grad_a_ref.shape[0]
    for left_ref, blocks, out_ref in ((left_a_ref, blocks_x, grad_a_ref), (left_b_ref, blocks_dy, grad_b_ref)):
        rows = jnp.concatenate([ref[...] for ref in blocks], axis=0)
        parts = lax.dot_general(left_ref[...], rows, FIRST, preferred_element_type=jnp.float32)
        proj = (parts[2 * rank :] + parts[rank : 2 * rank]) + parts[:rank]
        out_ref[...] = (factor * proj).astype(out_ref.dtype)


def grads(factor, left_a, left_b, blocks_x, blocks_dy, width):
    slots = left_a.shape[0]
    rank = left_a.shape[1] // 3
    chunk = min(width, CHUNK)
    left_spec = pl.BlockSpec((slots, 3 * rank), lambda i: (0, 0))
    rows_specs = [pl.BlockSpec((block.shape[0], chunk), lambda i: (0, i)) for block in blocks_x]
    out_spec = pl.BlockSpec((rank, chunk), lambda i: (0, i))
    return pl.pallas_call(
        lambda *refs: grads_kernel(len(blocks_x), *refs),
        grid=(width // chunk,),
        in_specs=[pl.BlockSpec(memory_space=pltpu.SMEM), left_spec, left_spec] + rows_specs * 2,
        out_specs=[out_spec, out_spec],
        out_shape=[jax.ShapeDtypeStruct((rank, width), jnp.bfloat16)] * 2,
        compiler_params=pltpu.CompilerParams(vmem_limit_bytes=VMEM_LIMIT),
        cost_estimate=pl.CostEstimate(
            flops=12 * slots * width * rank, bytes_accessed=4 * width * (slots + rank), transcendentals=0
        ),
    )(factor, left_a, left_b, *blocks_x, *blocks_dy)


def clip_factor(local_sq, adapters, rank, width):
    total = total_over_blk(local_sq[:1, :1])
    mean_sq = total / (2.0 * adapters * rank * width)
    return jnp.minimum(1.0, 1.0 / jnp.sqrt(mean_sq + EPS))


class Line:
    def __init__(self, window):
        self.window = window
        self.results = []

    def swap(self, value, partner):
        if len(self.results) >= self.window:
            value, _ = lax.optimization_barrier((value, self.results[-self.window]))
        size = lax.axis_size("blk")
        result = lax.ppermute(value, "blk", [(i, i ^ partner) for i in range(size)])
        self.results.append(result)
        return result


def per_device_blocks(tokens, cotangent, tenant, owner, down_factor_table, up_factor_table):
    rows, width = tokens.shape
    count_blk = lax.axis_size("blk")
    half = count_blk // 2
    adapters = owner.shape[0]
    rank = down_factor_table.shape[1]
    cap = 2 * rows // adapters
    down_weight = down_factor_table[0]
    up_weight = up_factor_table[0]
    me = lax.axis_index("blk").astype(jnp.int32)
    far, near = Line(FAR_WINDOW), Line(NEAR_WINDOW)
    low_of = lambda low, first, count: low[first * cap : (first + count) * cap]
    parts = rank // cap
    mirror_parts = []

    def send_weight(number):
        for _ in range(number):
            at = len(mirror_parts)
            mirror_parts.append(far.swap(down_weight[at * cap : (at + 1) * cap], half))

    send_weight(WEIGHT_FIRST)
    sent_dy = place(list(range(count_blk)), cap, me, owner, tenant, cotangent)
    others = [s for s in range(count_blk) if s != half]
    sent_x = dict(zip(others, place(others, cap, me, owner, tenant, tokens, with_live=True)))
    got_dy, got_x = {0: sent_dy[0]}, {0: sent_x[0]}
    near_queue = [(got_dy, sent_dy, s) for s in range(1, half)] + [(got_x, sent_x, s) for s in range(1, half)]
    for s in range(half, count_blk):
        got_dy[s] = far.swap(sent_dy[s], s)
        for got, sent, partner in near_queue[:RATE]:
            got[partner] = near.swap(sent[partner], partner)
        del near_queue[:RATE]
        if s == WEIGHT_MID:
            send_weight(1)
    for got, sent, partner in near_queue:
        got[partner] = near.swap(sent[partner], partner)
    send_weight(parts - len(mirror_parts))

    blocks_dy = [got_dy[s] for s in range(count_blk)]
    grad_hidden, gram_dy = rows_products(blocks_dy, up_weight, SCALE)
    (sent_mirror,) = place(
        [half], cap, me, owner, tenant, tokens, with_live=True, low=low_of(grad_hidden, half, half)
    )
    still = pl.BlockSpec((half * cap, rank), lambda i: (0, 0))
    own_back = back_rows(half, cap, low_of(grad_hidden, 0, half), down_weight, still, False)
    back = {0: own_back[0]}
    got_x[half + 1] = far.swap(sent_x[half + 1], half + 1)
    got_x[half] = far.swap(sent_mirror, half)
    for s in range(1, half // 2):
        got_x[half + 1 + s] = far.swap(sent_x[half + 1 + s], half + 1 + s)
        for at in (2 * s - 1, 2 * s):
            back[at] = near.swap(own_back[at], at)
    back[half - 1] = near.swap(own_back[half - 1], half - 1)
    mirror_low = pl.BlockSpec((cap, half * rank), lambda i: (0, width // (half * rank)))
    mirror_weight = jnp.concatenate(mirror_parts, axis=0)
    mirror_back = back_rows(half, cap, got_x[half], mirror_weight, mirror_low, True)
    back[half] = mirror_back[0]
    for at, s in enumerate(range(half + 1 + half // 2, count_blk)):
        got_x[s] = far.swap(sent_x[s], s)
        for partner in MIRROR_ORDER[2 * at : 2 * at + 2]:
            back[half + partner] = near.swap(mirror_back[partner], partner)
    for partner in MIRROR_ORDER[6:]:
        back[half + partner] = near.swap(mirror_back[partner], partner)

    blocks_x = [got_x[s] for s in range(count_blk)]
    hidden, gram_x, live = rows_products(blocks_x, down_weight, 1.0, with_extra=True)
    amount = jnp.sum(live[:, 0], dtype=jnp.float32).reshape(1, 1)
    left_a, left_b, local_sq = fold(amount, grad_hidden, gram_x, hidden, gram_dy)
    factor = clip_factor(local_sq, adapters, rank, width)
    grad_a, grad_b = grads(factor, left_a, left_b, blocks_x, blocks_dy, width)
    input_grad = input_grad_of(cap, me, owner, tenant, [back[s] for s in range(count_blk)])
    return (input_grad, grad_a[None], grad_b[None])


def per_device(tokens, cotangent, tenant, owner, down_factor_table, up_factor_table):
    rows, width = tokens.shape
    count_blk = lax.axis_size("blk")
    adapters = owner.shape[0]
    rank = down_factor_table.shape[1]
    cap = 2 * rows // adapters
    slots = count_blk * cap
    down_weight = down_factor_table[0]
    up_weight = up_factor_table[0]

    with jax.named_scope("targets"):
        tenant_ids = tenant[:, 0]
        match = tenant_ids[:, None] == jnp.arange(adapters, dtype=jnp.int32)[None, :]
        target_dev = jnp.sum(jnp.where(match, owner[None, :], 0), axis=1)
        row_ids = jnp.arange(rows, dtype=jnp.int32)
        same_before = (tenant_ids[:, None] == tenant_ids[None, :]) & (row_ids[None, :] < row_ids[:, None])
        position = jnp.sum(same_before.astype(jnp.int32), axis=1)
        target = target_dev * cap + position
        placing = (jnp.arange(slots, dtype=jnp.int32)[:, None] == target[None, :]).astype(jnp.bfloat16)

    def exchange(value):
        value = value.reshape(count_blk, cap, width)
        return lax.all_to_all(value, "blk", split_axis=0, concat_axis=0, tiled=True).reshape(slots, width)

    def place(value):
        return jnp.dot(placing, value, preferred_element_type=jnp.float32).astype(jnp.bfloat16)

    with jax.named_scope("send_cotangent"):
        rows_dy = exchange(place(cotangent))
    with jax.named_scope("send_tokens"):
        rows_x = exchange(place(tokens))
    with jax.named_scope("row_counts"):
        devices = jnp.arange(count_blk, dtype=jnp.int32)
        sent = jnp.sum((target_dev[:, None] == devices[None, :]).astype(jnp.float32), axis=0, keepdims=True)
        counts = total_over_blk(sent)
        amount = jnp.sum(jnp.where(devices == lax.axis_index("blk"), counts[0], 0.0)).reshape(1, 1)
    with jax.named_scope("grad_hidden"):
        grad_hidden, gram_dy = rows_products([rows_dy], up_weight, SCALE)
    with jax.named_scope("back"):
        back = jnp.dot(grad_hidden, down_weight, preferred_element_type=jnp.float32).astype(jnp.bfloat16)
        returned = exchange(back)
    with jax.named_scope("hidden"):
        hidden, gram_x = rows_products([rows_x], down_weight, 1.0)
    with jax.named_scope("fold"):
        left_a, left_b, local_sq = fold(amount, grad_hidden, gram_x, hidden, gram_dy)
    with jax.named_scope("clip"):
        factor = clip_factor(local_sq, adapters, rank, width)
    with jax.named_scope("grads"):
        grad_a, grad_b = grads(factor, left_a, left_b, [rows_x], [rows_dy], width)
    with jax.named_scope("input_grad"):
        input_grad = lax.dot_general(placing, returned, FIRST, preferred_element_type=jnp.float32).astype(
            jnp.bfloat16
        )
    return (input_grad, grad_a[None], grad_b[None])


def solution(mesh):
    body = per_device_blocks if mesh.shape["blk"] == 16 else per_device
    split = ("groups", "blk")
    in_specs = (P(split, None), P(split, None), P(split, None), P("groups"), P(split, None, None), P(split, None, None))
    out_specs = (P(split, None), P(split, None, None), P(split, None, None))
    return jax.shard_map(body, mesh=mesh, in_specs=in_specs, out_specs=out_specs, check_vma=False)
```

```python
import jax
import jax.numpy as jnp
from jax import lax
from jax.experimental import pallas as pl
from jax.experimental.pallas import tpu as pltpu
from jax.sharding import PartitionSpec as P

SCALE = 2.0
DAMPING = 1.0
EPS = 1e-06
VMEM_LIMIT = 44 * 1024 * 1024
LANES = 128
FAR_WINDOW = 4
CHUNK = 8192
WEIGHT_FIRST = 2
RATE = 1
WEIGHT_MID = 10
MIRROR_ORDER = [1, 2, 3, 4, 5, 6, 7]
NEAR_WINDOW = 4
LAST = (((1,), (1,)), ((), ()))
FIRST = (((0,), (0,)), ((), ()))


def total_over_blk(value):
    size = lax.axis_size("blk")
    if size & (size - 1):
        return lax.psum(value, "blk")
    step = 1
    while step < size:
        value = value + lax.ppermute(value, "blk", [(i, i ^ step) for i in range(size)])
        step *= 2
    return value


def rows_kernel(scale, count, with_extra, *refs):
    blocks, (weight_ref, low_ref, gram_ref, *rest) = refs[:count], refs[count:]
    low_total = rest[-1]
    step = pl.program_id(0)
    chunk = weight_ref.shape[1]

    @pl.when(step == 0)
    def _():
        low_total[...] = jnp.zeros_like(low_total)
        gram_ref[...] = jnp.zeros_like(gram_ref)
        if with_extra:
            rest[0][...] = jnp.concatenate([ref[:, ref.shape[1] - LANES :] for ref in blocks], axis=0)

    rows = jnp.concatenate([ref[:, :chunk] for ref in blocks], axis=0)
    low_total[...] += lax.dot_general(rows, weight_ref[...], LAST, preferred_element_type=jnp.float32)
    gram_ref[...] += lax.dot_general(rows, rows, LAST, preferred_element_type=jnp.float32)

    @pl.when(step == pl.num_programs(0) - 1)
    def _():
        low_ref[...] = (scale * low_total[...]).astype(low_ref.dtype)


def rows_products(blocks, weight, scale, with_extra=False):
    slots = sum(block.shape[0] for block in blocks)
    rank, width = weight.shape
    chunk = width if with_extra else min(width, CHUNK)
    in_specs = [
        pl.BlockSpec((block.shape[0], block.shape[1] if with_extra else chunk), lambda i: (0, i)) for block in blocks
    ]
    out_specs = [pl.BlockSpec((slots, rank), lambda i: (0, 0)), pl.BlockSpec((slots, slots), lambda i: (0, 0))]
    out_shape = [
        jax.ShapeDtypeStruct((slots, rank), jnp.bfloat16),
        jax.ShapeDtypeStruct((slots, slots), jnp.float32),
    ]
    if with_extra:
        out_specs.append(pl.BlockSpec((slots, LANES), lambda i: (0, 0)))
        out_shape.append(jax.ShapeDtypeStruct((slots, LANES), jnp.bfloat16))
    return pl.pallas_call(
        lambda *refs: rows_kernel(scale, len(blocks), with_extra, *refs),
        grid=(width // chunk,),
        in_specs=in_specs + [pl.BlockSpec((rank, chunk), lambda i: (0, i))],
        out_specs=out_specs,
        out_shape=out_shape,
        scratch_shapes=[pltpu.VMEM((slots, rank), jnp.float32)],
        compiler_params=pltpu.CompilerParams(vmem_limit_bytes=VMEM_LIMIT),
        cost_estimate=pl.CostEstimate(
            flops=2 * slots * width * (slots + rank),
            bytes_accessed=2 * width * (slots + rank),
            transcendentals=0,
        ),
    )(*blocks, weight)


def slot_targets(cap, me, owner_ref, column_ref, row_ref):
    column, row = column_ref[...], row_ref[...]
    rows, adapters = row.shape[1], owner_ref.shape[0]
    adapter = lax.broadcasted_iota(jnp.int32, (adapters, rows), 0)
    device = jnp.sum(jnp.where(adapter == row, owner_ref[...], 0), axis=0, keepdims=True)
    earlier = lax.broadcasted_iota(jnp.int32, (rows, rows), 0) < lax.broadcasted_iota(jnp.int32, (rows, rows), 1)
    position = jnp.sum(jnp.where((column == row) & earlier, 1, 0), axis=0, keepdims=True)
    partner = device ^ me
    return partner, partner * cap + position


def place_kernel(partners, cap, with_live, me_ref, owner_ref, column_ref, row_ref, values_ref, *refs):
    placing = refs[-1]
    low_refs, outs = refs[: len(refs) - 1 - len(partners)], refs[len(refs) - 1 - len(partners) : -1]
    step = pl.program_id(0)
    rows, chunk = row_ref.shape[1], values_ref.shape[1]

    @pl.when(step == 0)
    def _():
        _, target = slot_targets(cap, me_ref[0, 0], owner_ref, column_ref, row_ref)
        slot = lax.broadcasted_iota(jnp.int32, (cap, rows), 0)
        for at, partner in enumerate(partners):
            placing[at * cap : (at + 1) * cap, :] = jnp.where(slot + partner * cap == target, 1.0, 0.0).astype(
                placing.dtype
            )

    placed = jnp.dot(placing[...], values_ref[...], preferred_element_type=jnp.float32).astype(jnp.bfloat16)
    for at, out in enumerate(outs):
        if with_live:
            out[:, pl.ds(pl.multiple_of(step * chunk, chunk), chunk)] = placed[at * cap : (at + 1) * cap]
        else:
            out[...] = placed[at * cap : (at + 1) * cap]

    if with_live:

        @pl.when(step == pl.num_programs(0) - 1)
        def _():
            live = jnp.sum(placing[...].astype(jnp.float32), axis=1, keepdims=True).astype(jnp.bfloat16)
            for at, out in enumerate(outs):
                full = out.shape[1]
                out[:, full - LANES :] = jnp.broadcast_to(live[at * cap : (at + 1) * cap], (cap, LANES))
                if low_refs:
                    low = low_refs[0][...].astype(jnp.float32)
                    lanes = [low[q * cap : (q + 1) * cap] for q in range(low.shape[0] // cap)]
                    out[:, pl.num_programs(0) * chunk : full - LANES] = jnp.concatenate(lanes, axis=1).astype(
                        jnp.bfloat16
                    )


def place(partners, cap, me, owner, tenant, values, with_live=False, low=None):
    rows, width = values.shape
    adapters = owner.shape[0]
    full = width + (LANES if with_live else 0) + (low.size // cap if low is not None else 0)
    chunk = min(width, CHUNK)
    still = lambda shape: pl.BlockSpec(shape, lambda i: (0, 0))
    in_specs = [
        pl.BlockSpec(memory_space=pltpu.SMEM),
        still((adapters, 1)),
        still((rows, 1)),
        still((1, rows)),
        pl.BlockSpec((rows, chunk), lambda i: (0, i)),
    ]
    operands = [me.reshape(1, 1), owner.reshape(adapters, 1), tenant, tenant.reshape(1, rows), values]
    if low is not None:
        in_specs.append(still(low.shape))
        operands.append(low)
    out_spec = still((cap, full)) if with_live else pl.BlockSpec((cap, chunk), lambda i: (0, i))
    return pl.pallas_call(
        lambda *refs: place_kernel(partners, cap, with_live, *refs),
        grid=(width // chunk,),
        in_specs=in_specs,
        out_specs=[out_spec] * len(partners),
        out_shape=[jax.ShapeDtypeStruct((cap, full), jnp.bfloat16)] * len(partners),
        scratch_shapes=[pltpu.VMEM((len(partners) * cap, rows), jnp.bfloat16)],
        compiler_params=pltpu.CompilerParams(vmem_limit_bytes=VMEM_LIMIT),
        cost_estimate=pl.CostEstimate(
            flops=2 * len(partners) * cap * rows * width,
            bytes_accessed=2 * width * (rows + len(partners) * cap),
            transcendentals=0,
        ),
    )(*operands)


def back_kernel(count, stacked, low_ref, weight_ref, *outs):
    cap = outs[0].shape[0]
    rank = weight_ref.shape[0]
    if stacked:
        low = low_ref[...].astype(jnp.float32)
        low = jnp.concatenate([low[:, at * rank : (at + 1) * rank] for at in range(count)], axis=0)
        low = low.astype(jnp.bfloat16)
    else:
        low = low_ref[...]
    rows = jnp.dot(low, weight_ref[...], preferred_element_type=jnp.float32).astype(jnp.bfloat16)
    for at, out in enumerate(outs):
        out[...] = rows[at * cap : (at + 1) * cap]


def back_rows(count, cap, low, weight, low_spec, stacked):
    rank, width = weight.shape
    chunk = min(width, CHUNK)
    return pl.pallas_call(
        lambda *refs: back_kernel(count, stacked, *refs),
        grid=(width // chunk,),
        in_specs=[low_spec, pl.BlockSpec((rank, chunk), lambda i: (0, i))],
        out_specs=[pl.BlockSpec((cap, chunk), lambda i: (0, i))] * count,
        out_shape=[jax.ShapeDtypeStruct((cap, width), jnp.bfloat16)] * count,
        compiler_params=pltpu.CompilerParams(vmem_limit_bytes=VMEM_LIMIT),
        cost_estimate=pl.CostEstimate(
            flops=2 * count * cap * rank * width, bytes_accessed=2 * width * (rank + count * cap), transcendentals=0
        ),
    )(low, weight)


def input_grad_kernel(cap, count, me_ref, owner_ref, column_ref, row_ref, *refs):
    blocks, out_ref, placing = refs[:count], refs[count], refs[count + 1]
    step = pl.program_id(0)

    @pl.when(step == 0)
    def _():
        _, target = slot_targets(cap, me_ref[0, 0], owner_ref, column_ref, row_ref)
        slot = lax.broadcasted_iota(jnp.int32, placing.shape, 0)
        placing[...] = jnp.where(slot == target, 1.0, 0.0).astype(placing.dtype)

    returned = jnp.concatenate([ref[...] for ref in blocks], axis=0)
    out_ref[...] = lax.dot_general(placing[...], returned, FIRST, preferred_element_type=jnp.float32).astype(
        out_ref.dtype
    )


def input_grad_of(cap, me, owner, tenant, blocks):
    rows, adapters, count = tenant.shape[0], owner.shape[0], len(blocks)
    width = blocks[0].shape[1]
    chunk = min(width, CHUNK)
    still = lambda shape: pl.BlockSpec(shape, lambda i: (0, 0))
    return pl.pallas_call(
        lambda *refs: input_grad_kernel(cap, count, *refs),
        grid=(width // chunk,),
        in_specs=[
            pl.BlockSpec(memory_space=pltpu.SMEM),
            still((adapters, 1)),
            still((rows, 1)),
            still((1, rows)),
        ]
        + [pl.BlockSpec((cap, chunk), lambda i: (0, i))] * count,
        out_specs=pl.BlockSpec((rows, chunk), lambda i: (0, i)),
        out_shape=jax.ShapeDtypeStruct((rows, width), jnp.bfloat16),
        scratch_shapes=[pltpu.VMEM((count * cap, rows), jnp.bfloat16)],
        compiler_params=pltpu.CompilerParams(vmem_limit_bytes=VMEM_LIMIT),
        cost_estimate=pl.CostEstimate(
            flops=2 * rows * count * cap * width,
            bytes_accessed=2 * width * (rows + count * cap),
            transcendentals=0,
        ),
    )(me.reshape(1, 1), owner.reshape(adapters, 1), tenant, tenant.reshape(1, rows), *blocks)


def fold_one(low, gram, scale, amount):
    high = lax.Precision.HIGHEST
    low = low.astype(jnp.float32)
    slots = low.shape[0]
    left = jnp.sum(low, axis=0, keepdims=True) / amount
    raw = scale * low
    along = jnp.sum(raw * left, axis=1, keepdims=True)
    inner = raw - along * left / (DAMPING + jnp.sum(left * left))
    cross = jnp.sum(gram, axis=1, keepdims=True) / amount
    right_sq = jnp.sum(cross) / amount
    side = jnp.sum(inner * cross, axis=0, keepdims=True)
    factor = inner - side / (amount * (DAMPING + right_sq))
    spread = jnp.dot(gram, factor, precision=high, preferred_element_type=jnp.float32)
    return factor, jnp.sum(spread * factor)


def split3(value):
    first = value.astype(jnp.bfloat16)
    rest = value - first.astype(jnp.float32)
    second = rest.astype(jnp.bfloat16)
    third = (rest - second.astype(jnp.float32)).astype(jnp.bfloat16)
    return first, second, third


def fold_kernel(amount_ref, gh_ref, gram_x_ref, hidden_ref, gram_dy_ref, left_a_ref, left_b_ref, sq_ref):
    amount = amount_ref[0, 0]
    rank = gh_ref.shape[1]
    factor_a, sq_a = fold_one(gh_ref[...], gram_x_ref[...], 1.0, amount)
    factor_b, sq_b = fold_one(hidden_ref[...], gram_dy_ref[...], SCALE, amount)
    for out_ref, factor in ((left_a_ref, factor_a), (left_b_ref, factor_b)):
        for at, part in enumerate(split3(factor)):
            out_ref[:, at * rank : (at + 1) * rank] = part
    sq_ref[...] = jnp.zeros_like(sq_ref) + (sq_a + sq_b)


def fold(amount, grad_hidden, gram_x, hidden, gram_dy):
    slots, rank = hidden.shape
    whole = lambda shape: pl.BlockSpec(shape, lambda: (0, 0))
    return pl.pallas_call(
        fold_kernel,
        in_specs=[pl.BlockSpec(memory_space=pltpu.SMEM)]
        + [whole((slots, rank)), whole((slots, slots))] * 2,
        out_specs=[whole((slots, 3 * rank))] * 2 + [whole((8, 128))],
        out_shape=[jax.ShapeDtypeStruct((slots, 3 * rank), jnp.bfloat16)] * 2
        + [jax.ShapeDtypeStruct((8, 128), jnp.float32)],
        compiler_params=pltpu.CompilerParams(vmem_limit_bytes=VMEM_LIMIT),
        cost_estimate=pl.CostEstimate(
            flops=24 * slots * slots * rank, bytes_accessed=12 * slots * slots, transcendentals=0
        ),
    )(amount, grad_hidden, gram_x, hidden, gram_dy)


def grads_kernel(count, factor_ref, left_a_ref, left_b_ref, *refs):
    blocks_x, blocks_dy = refs[:count], refs[count : 2 * count]
    grad_a_ref, grad_b_ref = refs[2 * count :]
    factor = factor_ref[0, 0]
    rank = grad_a_ref.shape[0]
    for left_ref, blocks, out_ref in ((left_a_ref, blocks_x, grad_a_ref), (left_b_ref, blocks_dy, grad_b_ref)):
        rows = jnp.concatenate([ref[...] for ref in blocks], axis=0)
        parts = lax.dot_general(left_ref[...], rows, FIRST, preferred_element_type=jnp.float32)
        proj = (parts[2 * rank :] + parts[rank : 2 * rank]) + parts[:rank]
        out_ref[...] = (factor * proj).astype(out_ref.dtype)


def grads(factor, left_a, left_b, blocks_x, blocks_dy, width):
    slots = left_a.shape[0]
    rank = left_a.shape[1] // 3
    chunk = min(width, CHUNK)
    left_spec = pl.BlockSpec((slots, 3 * rank), lambda i: (0, 0))
    rows_specs = [pl.BlockSpec((block.shape[0], chunk), lambda i: (0, i)) for block in blocks_x]
    out_spec = pl.BlockSpec((rank, chunk), lambda i: (0, i))
    return pl.pallas_call(
        lambda *refs: grads_kernel(len(blocks_x), *refs),
        grid=(width // chunk,),
        in_specs=[pl.BlockSpec(memory_space=pltpu.SMEM), left_spec, left_spec] + rows_specs * 2,
        out_specs=[out_spec, out_spec],
        out_shape=[jax.ShapeDtypeStruct((rank, width), jnp.bfloat16)] * 2,
        compiler_params=pltpu.CompilerParams(vmem_limit_bytes=VMEM_LIMIT),
        cost_estimate=pl.CostEstimate(
            flops=12 * slots * width * rank, bytes_accessed=4 * width * (slots + rank), transcendentals=0
        ),
    )(factor, left_a, left_b, *blocks_x, *blocks_dy)


def clip_factor(local_sq, adapters, rank, width):
    total = total_over_blk(local_sq[:1, :1])
    mean_sq = total / (2.0 * adapters * rank * width)
    return jnp.minimum(1.0, 1.0 / jnp.sqrt(mean_sq + EPS))


class Line:
    def __init__(self, window):
        self.window = window
        self.results = []

    def swap(self, value, partner):
        if len(self.results) >= self.window:
            value, _ = lax.optimization_barrier((value, self.results[-self.window]))
        size = lax.axis_size("blk")
        result = lax.ppermute(value, "blk", [(i, i ^ partner) for i in range(size)])
        self.results.append(result)
        return result


def per_device_blocks(tokens, cotangent, tenant, owner, down_factor_table, up_factor_table):
    rows, width = tokens.shape
    count_blk = lax.axis_size("blk")
    half = count_blk // 2
    adapters = owner.shape[0]
    rank = down_factor_table.shape[1]
    cap = 2 * rows // adapters
    down_weight = down_factor_table[0]
    up_weight = up_factor_table[0]
    me = lax.axis_index("blk").astype(jnp.int32)
    far, near = Line(FAR_WINDOW), Line(NEAR_WINDOW)
    low_of = lambda low, first, count: low[first * cap : (first + count) * cap]
    parts = rank // cap
    mirror_parts = []

    def send_weight(number):
        for _ in range(number):
            at = len(mirror_parts)
            mirror_parts.append(far.swap(down_weight[at * cap : (at + 1) * cap], half))

    send_weight(WEIGHT_FIRST)
    sent_dy = place(list(range(count_blk)), cap, me, owner, tenant, cotangent)
    others = [s for s in range(count_blk) if s != half]
    sent_x = dict(zip(others, place(others, cap, me, owner, tenant, tokens, with_live=True)))
    got_dy, got_x = {0: sent_dy[0]}, {0: sent_x[0]}
    near_queue = [(got_dy, sent_dy, s) for s in range(1, half)] + [(got_x, sent_x, s) for s in range(1, half)]
    for s in range(half, count_blk):
        got_dy[s] = far.swap(sent_dy[s], s)
        for got, sent, partner in near_queue[:RATE]:
            got[partner] = near.swap(sent[partner], partner)
        del near_queue[:RATE]
        if s == WEIGHT_MID:
            send_weight(1)
    for got, sent, partner in near_queue:
        got[partner] = near.swap(sent[partner], partner)
    send_weight(parts - len(mirror_parts))

    blocks_dy = [got_dy[s] for s in range(count_blk)]
    grad_hidden, gram_dy = rows_products(blocks_dy, up_weight, SCALE)
    (sent_mirror,) = place(
        [half], cap, me, owner, tenant, tokens, with_live=True, low=low_of(grad_hidden, half, half)
    )
    still = pl.BlockSpec((half * cap, rank), lambda i: (0, 0))
    own_back = back_rows(half, cap, low_of(grad_hidden, 0, half), down_weight, still, False)
    back = {0: own_back[0]}
    got_x[half + 1] = far.swap(sent_x[half + 1], half + 1)
    got_x[half] = far.swap(sent_mirror, half)
    for s in range(1, half // 2):
        got_x[half + 1 + s] = far.swap(sent_x[half + 1 + s], half + 1 + s)
        for at in (2 * s - 1, 2 * s):
            back[at] = near.swap(own_back[at], at)
    back[half - 1] = near.swap(own_back[half - 1], half - 1)
    mirror_low = pl.BlockSpec((cap, half * rank), lambda i: (0, width // (half * rank)))
    mirror_weight = jnp.concatenate(mirror_parts, axis=0)
    mirror_back = back_rows(half, cap, got_x[half], mirror_weight, mirror_low, True)
    back[half] = mirror_back[0]
    for at, s in enumerate(range(half + 1 + half // 2, count_blk)):
        got_x[s] = far.swap(sent_x[s], s)
        for partner in MIRROR_ORDER[2 * at : 2 * at + 2]:
            back[half + partner] = near.swap(mirror_back[partner], partner)
    for partner in MIRROR_ORDER[6:]:
        back[half + partner] = near.swap(mirror_back[partner], partner)

    blocks_x = [got_x[s] for s in range(count_blk)]
    hidden, gram_x, live = rows_products(blocks_x, down_weight, 1.0, with_extra=True)
    amount = jnp.sum(live[:, 0], dtype=jnp.float32).reshape(1, 1)
    left_a, left_b, local_sq = fold(amount, grad_hidden, gram_x, hidden, gram_dy)
    factor = clip_factor(local_sq, adapters, rank, width)
    grad_a, grad_b = grads(factor, left_a, left_b, blocks_x, blocks_dy, width)
    input_grad = input_grad_of(cap, me, owner, tenant, [back[s] for s in range(count_blk)])
    return (input_grad, grad_a[None], grad_b[None])


def per_device(tokens, cotangent, tenant, owner, down_factor_table, up_factor_table):
    rows, width = tokens.shape
    count_blk = lax.axis_size("blk")
    adapters = owner.shape[0]
    rank = down_factor_table.shape[1]
    cap = 2 * rows // adapters
    slots = count_blk * cap
    down_weight = down_factor_table[0]
    up_weight = up_factor_table[0]

    with jax.named_scope("targets"):
        tenant_ids = tenant[:, 0]
        match = tenant_ids[:, None] == jnp.arange(adapters, dtype=jnp.int32)[None, :]
        target_dev = jnp.sum(jnp.where(match, owner[None, :], 0), axis=1)
        row_ids = jnp.arange(rows, dtype=jnp.int32)
        same_before = (tenant_ids[:, None] == tenant_ids[None, :]) & (row_ids[None, :] < row_ids[:, None])
        position = jnp.sum(same_before.astype(jnp.int32), axis=1)
        target = target_dev * cap + position
        placing = (jnp.arange(slots, dtype=jnp.int32)[:, None] == target[None, :]).astype(jnp.bfloat16)

    def exchange(value):
        value = value.reshape(count_blk, cap, width)
        return lax.all_to_all(value, "blk", split_axis=0, concat_axis=0, tiled=True).reshape(slots, width)

    def place(value):
        return jnp.dot(placing, value, preferred_element_type=jnp.float32).astype(jnp.bfloat16)

    with jax.named_scope("send_cotangent"):
        rows_dy = exchange(place(cotangent))
    with jax.named_scope("send_tokens"):
        rows_x = exchange(place(tokens))
    with jax.named_scope("row_counts"):
        devices = jnp.arange(count_blk, dtype=jnp.int32)
        sent = jnp.sum((target_dev[:, None] == devices[None, :]).astype(jnp.float32), axis=0, keepdims=True)
        counts = total_over_blk(sent)
        amount = jnp.sum(jnp.where(devices == lax.axis_index("blk"), counts[0], 0.0)).reshape(1, 1)
    with jax.named_scope("grad_hidden"):
        grad_hidden, gram_dy = rows_products([rows_dy], up_weight, SCALE)
    with jax.named_scope("back"):
        back = jnp.dot(grad_hidden, down_weight, preferred_element_type=jnp.float32).astype(jnp.bfloat16)
        returned = exchange(back)
    with jax.named_scope("hidden"):
        hidden, gram_x = rows_products([rows_x], down_weight, 1.0)
    with jax.named_scope("fold"):
        left_a, left_b, local_sq = fold(amount, grad_hidden, gram_x, hidden, gram_dy)
    with jax.named_scope("clip"):
        factor = clip_factor(local_sq, adapters, rank, width)
    with jax.named_scope("grads"):
        grad_a, grad_b = grads(factor, left_a, left_b, [rows_x], [rows_dy], width)
    with jax.named_scope("input_grad"):
        input_grad = lax.dot_general(placing, returned, FIRST, preferred_element_type=jnp.float32).astype(
            jnp.bfloat16
        )
    return (input_grad, grad_a[None], grad_b[None])


def solution(mesh):
    body = per_device_blocks if mesh.shape["blk"] == 16 else per_device
    split = ("groups", "blk")
    in_specs = (P(split, None), P(split, None), P(split, None), P("groups"), P(split, None, None), P(split, None, None))
    out_specs = (P(split, None), P(split, None, None), P(split, None, None))
    return jax.shard_map(body, mesh=mesh, in_specs=in_specs, out_specs=out_specs, check_vma=False)
```
